512 devices in a mesh: ctx: 16 (over y, x_lo), fsdp: 32 (over z, x_hi, core).
Axes of the slice: x: 4 (x_hi: 2, x_lo: 2; x = x_hi * 2 + x_lo), y: 8, z: 8, core: 2. Of those that a mesh axis runs over, the one named last changes fastest.
Arguments:
- asking_vectors_stacked: bfloat16 [65536, 2048], P(('ctx', 'fsdp')), may hold values from -10 to 10
- lookup_vectors_stacked: bfloat16 [65536, 256], P(('ctx', 'fsdp')), may hold values from -10 to 10
- content_vectors_stacked: bfloat16 [65536, 256], P(('ctx', 'fsdp')), may hold values from -6 to 6
- passage_label: int32 [65536], P(('ctx', 'fsdp')), may hold values from 0 to 511, never falling along the last dimension, each value on 1 to 256 neighbouring positions
- skip_path_derivative: bfloat16 [65536, 1440], P(('ctx', 'fsdp')), may hold values from -6 to 6
- specialist_entry_activations: bfloat16 [65536, 1440], P(('ctx', 'fsdp')), may hold values from -6 to 6
- merged_activation_derivative: bfloat16 [65536, 1440], P(('ctx', 'fsdp')), may hold values from -6 to 6
- picked_specialist_ids: int32 [65536, 4], P(('ctx', 'fsdp')), may hold values from 0 to 127, all different within a row; in each aligned block of 128 rows (0 to 127, 128 to 255, ...) at most 6 rows name the same one
- dispatcher_mixing_factor: bfloat16 [65536, 4], P(('ctx', 'fsdp')), may hold values from 0.099609375 to 1
- retained_specialist_ids: int32 [96], replicated, may hold values from 0 to 127, as said below
- specialist_linear_map: bfloat16 [16, 1440, 1440], P('ctx', 'fsdp'), may hold values from -0.15625 to 0.15625
- attention_final_linear_map: bfloat16 [2048, 1440], P('fsdp'), may hold values from -0.15625 to 0.15625
Outputs:
- query_grad: bfloat16 [65536, 2048], P(('ctx', 'fsdp'))
- key_grad: bfloat16 [65536, 256], P(('ctx', 'fsdp'))
- value_grad: bfloat16 [65536, 256], P(('ctx', 'fsdp'))
- specialist_source_derivative: bfloat16 [65536, 1440], P(('ctx', 'fsdp'))
- dispatcher_factor_derivative: bfloat16 [65536, 4], P(('ctx', 'fsdp'))
- specialist_map_derivative: bfloat16 [16, 1440, 1440], P('ctx', 'fsdp')
The draws below stay inside these ranges and needn't reach their ends.
Inputs may be any that keep to these rules, and one draw needn't show every extreme that they name: `passage_label`: document numbers never fall along the sequence; each document holds 1 to 256 positions and one holds exactly 256. `picked_specialist_ids`: each row names 4 different experts; among the 128 rows of one device no expert is named by more than 6 rows, a bound that some block reaches. `retained_specialist_ids`: 96 different expert numbers.
All inputs are finite; a program needn't handle non-finite values.
Results may differ from the reference program's by a relative error of at most 0.024.
Values may be sent and summed in bfloat16 or wider, within the bound.
No kernel may reach another device: no remote copies, remote signals or barrier semaphores. Data moves between devices by JAX's collectives and lax.ppermute only.
A program may use at most 64 MiB of HBM per device.

```python
import math
import jax
import jax.numpy as jnp
import numpy as np
from jax import lax

TOK_DEV = 128
HEADS = 32
KV_HEADS = 4
HEAD_DIM = 64
D = 1440
F = 1440
ROUTER_EXPERTS = 128
PRUNED_EXPERTS = 96
TOPK = 4
GROUP = 8
LENGTH = 65536
DOCS = 512
DOC_MOST = 256
CAP = 6
LOADED_SPECIALS = 16
N_CTX = 16
N_FSDP = 32


def draw_lookup_vectors_stacked(key, part):
    key = jax.random.fold_in(key, 3)
    values = jax.random.normal(key, (LENGTH, KV_HEADS * HEAD_DIM), jnp.float32)
    return jnp.clip(values, -10.0, 10.0).astype(jnp.bfloat16)


def draw_asking_vectors_stacked(key, part):
    key = jax.random.fold_in(key, 11)
    values = jax.random.normal(key, (LENGTH, HEADS * HEAD_DIM), jnp.float32)
    return jnp.clip(values, -10.0, 10.0).astype(jnp.bfloat16)


def draw_retained_specialist_ids(key, part):
    key = jax.random.fold_in(key, 5)
    return jax.random.permutation(key, ROUTER_EXPERTS)[:PRUNED_EXPERTS].astype(jnp.int32)


def steps_of(own_key, shape, split, smallest, high):
    factor_of, own = 1.0, jax.random.fold_in(own_key, 6)
    for axis_at, blocks in split:
        draws = jnp.exp(jax.random.uniform(jax.random.fold_in(own, axis_at), (blocks,), jnp.float32, smallest / len(split), high / len(split)))
        factor_of = factor_of * jnp.repeat(draws, shape[axis_at] // blocks).reshape([-1 if axis == axis_at else 1 for axis in range(len(shape))])
    return factor_of


def length_profile(count, total, limit, skew):
    portions = [(1 << 20) // math.isqrt(grade ** skew) + 1 for grade in range(2, count + 1)]
    surplus, given = total - limit - (count - 1), [1] * (count - 1)
    while surplus > 0:
        movable = [i for i in range(count - 1) if given[i] < limit]
        whole, remaining = sum([portions[i] for i in movable]), surplus
        for i in movable:
            more = min(limit - given[i], max(1, remaining * portions[i] // whole), surplus)
            given[i] = given[i] + more
            surplus = surplus - more
    return np.array([limit] + given)


def ragged(key, count, total, most, skew):
    if count == 2:
        one = jax.random.randint(key, (), max(1, total - most), min(most, total - 1) + 1)
        return jnp.stack([one, total - one])
    tallies = jnp.asarray(length_profile(count, total, most, skew), jnp.int32)
    pairs = (count - 1) // 2
    source_of, taker = tallies[1:1 + 2 * pairs:2], tallies[2:2 + 2 * pairs:2]
    room = jnp.minimum(source_of - 1, most - taker)
    shifted = jax.random.randint(jax.random.fold_in(key, 1), (pairs,), 0, 1 << 20) % (room + 1)
    tallies = tallies.at[1:1 + 2 * pairs:2].set(source_of - shifted).at[2:2 + 2 * pairs:2].set(taker + shifted)
    return tallies[jax.random.permutation(jax.random.fold_in(key, 2), count)]


def assign_block(stream_key, own, number, rows, amount, top, reach, lean):
    ranking = jax.random.permutation(stream_key, amount)
    heavy_load, ordinary = load_shares(amount, rows * top, reach, lean, True), load_shares(amount, rows * top, reach, lean, False)
    places = jnp.arange(amount)

    def named(lengths, offset_by):
        used = int((lengths > 0).sum())
        fixed = max(1, used // 4)
        passed = fixed + (places - fixed + offset_by * (used - fixed)) % max(1, amount - fixed)
        return jnp.zeros((amount,), jnp.int32).at[ranking[jnp.where(places < fixed, places, passed)]].set(jnp.asarray(lengths, jnp.int32))

    lengths = jnp.where(number % 4 == 0, named(heavy_load, number // 4), named(ordinary, number - number // 4 - 1))
    mixed = jax.random.permutation(jax.random.fold_in(own, 3), amount)
    donor, receiver = mixed[0:amount // 2 * 2:2], mixed[1:amount // 2 * 2:2]
    room = jnp.minimum(lengths[donor] - 1, reach - lengths[receiver]) // 2
    room = jnp.where((donor == ranking[0]) | (receiver == ranking[0]) | (lengths[receiver] == 0), 0, jnp.maximum(room, 0))
    passed = jax.random.randint(jax.random.fold_in(own, 4), (amount // 2,), 0, 1 << 20) % (room + 1)
    lengths = lengths.at[donor].add(-passed).at[receiver].add(passed)
    members = jnp.searchsorted(jnp.cumsum(lengths), jnp.arange(rows * top), side="right").astype(jnp.int32)
    table = members.reshape(top, rows).T
    table = table[jax.random.permutation(jax.random.fold_in(own, 1), rows)]
    offset_by = jax.random.randint(jax.random.fold_in(own, 2), (rows, 1), 0, top)
    return jnp.take_along_axis(table, (jnp.arange(top)[None, :] + offset_by) % top, axis=1)


def load_shares(count, total, bound, lean, full):
    weights = [(1 << 20) // math.isqrt(grade ** lean) + 1 for grade in range(1, count + 1)]
    largest = bound if full else min(bound, max(-(-total // count), total * weights[0] // sum(weights)))
    least = 1 if total - largest >= count - 1 else 0
    holding, surplus = [largest] + [least] * (count - 1), total - largest - least * (count - 1)
    while surplus > 0:
        candidates = [i for i in range(1, count) if holding[i] < largest] or [i for i in range(1, count) if holding[i] < bound]
        mass, remaining = sum([weights[i] for i in candidates]), surplus
        for i in candidates:
            addition = min(bound - holding[i], max(1, remaining * weights[i] // mass), surplus)
            holding[i] = holding[i] + addition
            surplus = surplus - addition
    return np.array(holding)


def scatter_about(key, extent, deviation, reach, split=(), kind=jnp.bfloat16):
    level = steps_of(key, extent, split, -0.22, 0.18) if split else 1.0
    values = jax.random.normal(key, extent, jnp.float32) * deviation * level
    return jnp.minimum(jnp.maximum(values, -reach), reach).astype(kind)


def setup_inputs(seed: int = 0) -> dict:
    key_list = jax.random.split(jax.random.key(seed), 13)
    asking_vectors_stacked = draw_asking_vectors_stacked(jax.random.fold_in(key_list[12], 71), 0)
    lookup_vectors_stacked = draw_lookup_vectors_stacked(jax.random.fold_in(key_list[12], 71), 0)
    content_vectors_stacked = scatter_about(key_list[2], (LENGTH, KV_HEADS * HEAD_DIM), 1.0, 6.0, ((0, 512),))
    passage_label = jnp.searchsorted(jnp.cumsum(ragged(key_list[3], DOCS, LENGTH, DOC_MOST, 1)), jnp.arange(LENGTH), side="right").astype(jnp.int32)
    skip_path_derivative = scatter_about(key_list[4], (LENGTH, D), 1.0, 6.0, ((0, 512),))
    specialist_entry_activations = scatter_about(key_list[5], (LENGTH, D), 1.0, 6.0, ((0, 512),))
    merged_activation_derivative = scatter_about(key_list[6], (LENGTH, F), 1.0, 6.0, ((0, 512),))
    picked_specialist_ids_keys = jax.random.split(jax.random.fold_in(key_list[7], 1), LENGTH // TOK_DEV)
    picked_specialist_ids_turns = jax.random.permutation(jax.random.fold_in(key_list[7], 3), LENGTH // TOK_DEV)
    picked_specialist_ids = jax.vmap(lambda own, number: assign_block(jax.random.fold_in(key_list[7], 2), own, number, TOK_DEV, ROUTER_EXPERTS, TOPK, CAP, 2))(picked_specialist_ids_keys, picked_specialist_ids_turns).reshape((LENGTH, TOPK))
    dispatcher_mixing_factor = jnp.clip(0.099609375 + 0.9003906 * jax.random.uniform(key_list[8], (LENGTH, TOPK), jnp.float32) ** steps_of(key_list[8], (LENGTH, TOPK), ((0, 512),), -0.2, 0.2), 0.099609375, 1.0).astype(jnp.bfloat16)
    retained_specialist_ids = draw_retained_specialist_ids(jax.random.fold_in(key_list[12], 71), 0)
    specialist_linear_map = scatter_about(key_list[10], (LOADED_SPECIALS, D, F), D ** -0.5, 0.15625, ((0, 16), (1, 32)))
    attention_final_linear_map = scatter_about(key_list[11], (HEADS * HEAD_DIM, D), D ** -0.5, 0.15625, ((0, 32),))
    return {"asking_vectors_stacked": asking_vectors_stacked, "lookup_vectors_stacked": lookup_vectors_stacked, "content_vectors_stacked": content_vectors_stacked, "passage_label": passage_label, "skip_path_derivative": skip_path_derivative, "specialist_entry_activations": specialist_entry_activations, "merged_activation_derivative": merged_activation_derivative, "picked_specialist_ids": picked_specialist_ids, "dispatcher_mixing_factor": dispatcher_mixing_factor, "retained_specialist_ids": retained_specialist_ids, "specialist_linear_map": specialist_linear_map, "attention_final_linear_map": attention_final_linear_map}


def group_terms(queries, keys_win, values_win, grads_in, allowed, scale):
    queries = queries.astype(jnp.float32)
    keys_win = keys_win.astype(jnp.float32)
    values_win = values_win.astype(jnp.float32)
    grads_in = grads_in.astype(jnp.float32)
    scores = jnp.einsum("tgd,kd->gtk", queries, keys_win) * scale
    scores = jnp.where(allowed[None], scores, -1e30)
    highest = jnp.max(scores, axis=-1, keepdims=True)
    raised = jnp.where(allowed[None], jnp.exp(scores - highest), 0.0)
    shares = raised / jnp.sum(raised, axis=-1, keepdims=True)
    shares_low = lax.optimization_barrier(shares.astype(jnp.bfloat16)).astype(jnp.float32)
    attended = jnp.einsum("gtk,kd->tgd", shares_low, values_win)
    centre = jnp.sum(grads_in * attended, axis=-1)
    share_grad = jnp.einsum("tgd,kd->gtk", grads_in, values_win)
    score_grad = shares * (share_grad - centre.T[:, :, None]) * scale
    score_grad = lax.optimization_barrier(score_grad.astype(jnp.bfloat16)).astype(jnp.float32)
    query_part = jnp.einsum("gtk,kd->tgd", score_grad, keys_win).astype(jnp.bfloat16)
    key_part = jnp.einsum("gtk,tgd->kd", score_grad, queries)
    value_part = jnp.einsum("gtk,tgd->kd", shares_low, grads_in)
    return query_part, key_part, value_part


def attention_grads(asking_vectors_stacked, lookup_vectors_stacked, content_vectors_stacked, passage_label, attn_cotangent):
    blocks = LENGTH // TOK_DEV
    width = KV_HEADS * HEAD_DIM
    scale = HEAD_DIM ** -0.5
    key_pad = jnp.concatenate([jnp.zeros((2 * TOK_DEV, width), lookup_vectors_stacked.dtype), lookup_vectors_stacked], axis=0)
    value_pad = jnp.concatenate([jnp.zeros((2 * TOK_DEV, width), content_vectors_stacked.dtype), content_vectors_stacked], axis=0)
    doc_pad = jnp.concatenate([jnp.full((2 * TOK_DEV,), -1, jnp.int32), passage_label.astype(jnp.int32)], axis=0)
    window_index = jnp.arange(3 * TOK_DEV, dtype=jnp.int32)
    query_index = jnp.arange(TOK_DEV, dtype=jnp.int32)
    causal = window_index[None, :] <= 2 * TOK_DEV + query_index[:, None]

    def one_block(block):
        start_position_shift = (block * TOK_DEV).astype(jnp.int32)
        queries = lax.dynamic_slice_in_dim(asking_vectors_stacked, start_position_shift, TOK_DEV, 0).reshape(TOK_DEV, KV_HEADS, GROUP, HEAD_DIM)
        grads_in = lax.dynamic_slice_in_dim(attn_cotangent, start_position_shift, TOK_DEV, 0).reshape(TOK_DEV, KV_HEADS, GROUP, HEAD_DIM)
        keys_win = lax.dynamic_slice_in_dim(key_pad, start_position_shift, 3 * TOK_DEV, 0).reshape(3 * TOK_DEV, KV_HEADS, HEAD_DIM)
        values_win = lax.dynamic_slice_in_dim(value_pad, start_position_shift, 3 * TOK_DEV, 0).reshape(3 * TOK_DEV, KV_HEADS, HEAD_DIM)
        own_docs = lax.dynamic_slice_in_dim(passage_label.astype(jnp.int32), start_position_shift, TOK_DEV, 0)
        near_docs = lax.dynamic_slice_in_dim(doc_pad, start_position_shift, 3 * TOK_DEV, 0)
        allowed = causal & (near_docs[None, :] == own_docs[:, None])
        query_part, key_part, value_part = jax.vmap(group_terms, in_axes=(1, 1, 1, 1, None, None))(
            queries, keys_win, values_win, grads_in, allowed, scale)
        query_part = query_part.transpose(1, 0, 2, 3).reshape(TOK_DEV, HEADS * HEAD_DIM)
        key_part = key_part.transpose(1, 0, 2).reshape(3 * TOK_DEV, width)
        value_part = value_part.transpose(1, 0, 2).reshape(3 * TOK_DEV, width)
        return query_part, key_part, value_part

    query_all, key_parts, value_parts = lax.map(one_block, jnp.arange(blocks, dtype=jnp.int32))

    def settle(parts):
        parts = parts.reshape(blocks, 3, TOK_DEV, width)
        after_one = jnp.concatenate([parts[1:, 1], jnp.zeros((1, TOK_DEV, width), jnp.float32)], axis=0)
        after_two = jnp.concatenate([parts[2:, 0], jnp.zeros((2, TOK_DEV, width), jnp.float32)], axis=0)
        total = parts[:, 2] + after_one + after_two
        return total.reshape(LENGTH, width).astype(jnp.bfloat16)

    return query_all.reshape(LENGTH, HEADS * HEAD_DIM), settle(key_parts), settle(value_parts)


def specialist_derivative(specialist_entry_activations, merged_activation_derivative, picked_specialist_ids, dispatcher_mixing_factor, retained_specialist_ids, specialist_linear_map):
    blocks = LENGTH // TOK_DEV
    slots = jnp.arange(CAP, dtype=jnp.int32)
    inputs_blocked = specialist_entry_activations.astype(jnp.float32).reshape(blocks, TOK_DEV, D)
    grads_blocked = merged_activation_derivative.astype(jnp.float32).reshape(blocks, TOK_DEV, F)
    gate_values = dispatcher_mixing_factor.astype(jnp.float32)

    def lone_specialist(carry, pieces):
        input_total, gate_total = carry
        weight_one, expert_id = pieces
        chosen = picked_specialist_ids == expert_id
        routed = jnp.any(chosen, axis=-1).astype(jnp.int32).reshape(blocks, TOK_DEV)
        gating = jnp.sum(jnp.where(chosen, gate_values, 0.0), axis=-1).reshape(blocks, TOK_DEV)
        ranks = jnp.cumsum(routed, axis=1) - 1
        dispatch = ((ranks[:, None, :] == slots[None, :, None]) & (routed[:, None, :] == 1)).astype(jnp.float32)
        in_rows = jnp.einsum("bct,btd->bcd", dispatch, inputs_blocked).astype(jnp.bfloat16).reshape(-1, D)
        grad_rows = jnp.einsum("bct,btn->bcn", dispatch, grads_blocked).reshape(-1, F)
        gate_rows = jnp.einsum("bct,bt->bc", dispatch, gating).reshape(-1)
        pre = jnp.dot(in_rows, weight_one, preferred_element_type=jnp.float32)
        activated = jax.nn.silu(pre)
        gate_part = lax.optimization_barrier(jnp.sum(grad_rows * activated, axis=-1).astype(jnp.bfloat16))
        sigma = jax.nn.sigmoid(pre)
        slope = sigma * (1.0 + pre * (1.0 - sigma))
        pre_grad = lax.optimization_barrier((gate_rows[:, None] * grad_rows * slope).astype(jnp.bfloat16))
        row_grads = lax.optimization_barrier(
            jnp.dot(pre_grad, weight_one.T, preferred_element_type=jnp.float32).astype(jnp.bfloat16))
        partial_value = jnp.einsum("cfkd,cfkn->fdn",
                             in_rows.astype(jnp.float32).reshape(N_CTX, N_FSDP, CAP, D),
                             pre_grad.astype(jnp.float32).reshape(N_CTX, N_FSDP, CAP, F))
        partial_value = lax.optimization_barrier(partial_value.astype(jnp.bfloat16)).astype(jnp.float32)
        specialist_map_derivative = jnp.sum(partial_value, axis=0).astype(jnp.bfloat16)
        input_part = jnp.einsum("bct,bcd->btd", dispatch,
                                row_grads.astype(jnp.float32).reshape(blocks, CAP, D)).reshape(LENGTH, D)
        per_token = jnp.einsum("bct,bc->bt", dispatch,
                               gate_part.astype(jnp.float32).reshape(blocks, CAP)).reshape(LENGTH)
        gate_total = gate_total + jnp.where(chosen, per_token[:, None], 0.0)
        return (input_total + input_part, gate_total), specialist_map_derivative

    start_position_shift = (jnp.zeros((LENGTH, D), jnp.float32), jnp.zeros((LENGTH, TOPK), jnp.float32))
    (input_total, gate_total), weight_grads = lax.scan(
        lone_specialist, start_position_shift, (specialist_linear_map, retained_specialist_ids[:LOADED_SPECIALS].astype(jnp.int32)))
    return input_total.astype(jnp.bfloat16), gate_total.astype(jnp.bfloat16), weight_grads


def reference(asking_vectors_stacked, lookup_vectors_stacked, content_vectors_stacked, passage_label, skip_path_derivative, specialist_entry_activations, merged_activation_derivative,
              picked_specialist_ids, dispatcher_mixing_factor, retained_specialist_ids, specialist_linear_map, attention_final_linear_map):
    specialist_source_derivative, dispatcher_factor_derivative, specialist_map_derivative = specialist_derivative(specialist_entry_activations, merged_activation_derivative, picked_specialist_ids, dispatcher_mixing_factor, retained_specialist_ids,
                                                      specialist_linear_map)
    hidden_grad = (skip_path_derivative.astype(jnp.float32) + specialist_source_derivative.astype(jnp.float32)).astype(jnp.bfloat16)
    attn_cotangent = lax.dot_general(hidden_grad, attention_final_linear_map, (((1,), (1,)), ((), ())),
                                     preferred_element_type=jnp.float32).astype(jnp.bfloat16)
    query_grad, key_grad, value_grad = attention_grads(asking_vectors_stacked, lookup_vectors_stacked, content_vectors_stacked, passage_label, attn_cotangent)
    return (query_grad, key_grad, value_grad, specialist_source_derivative, dispatcher_factor_derivative, specialist_map_derivative)
```

```python
import jax
import jax.numpy as jnp
from jax import lax
from jax.experimental import pallas as pl
from jax.experimental.pallas import tpu as pltpu
from jax.sharding import Mesh, PartitionSpec as P

TOK = 128
D = 1440
F = 1440
HEADS = 32
KV_HEADS = 4
HD = 64
CAP = 6
CAPP = 8
EXPERTS = 16
ROWS = EXPERTS * CAPP
SEG = 48
SHARD = 45
DP = 1536
HALF = 768
SEND = 3072
BACK = 1664
KV = 256
WIDE = 640
BF = jnp.bfloat16
F32 = jnp.float32
ALL = ("y", "xl", "z", "xh", "core")
CTX = ("y", "xl")
SWAP = ((0, 1), (1, 0))


def dot(a, b, dims):
    return lax.dot_general(a, b, (dims, ((), ())), preferred_element_type=F32)


def spec_vmem():
    return pl.BlockSpec(memory_space=pltpu.VMEM)


def spec_smem():
    return pl.BlockSpec(memory_space=pltpu.SMEM)


def call(kernel, outs, scratch, flops, nbytes, n_smem, n_vmem):
    return pl.pallas_call(
        kernel,
        out_shape=outs,
        in_specs=[spec_smem()] * n_smem + [spec_vmem()] * n_vmem,
        out_specs=[spec_vmem()] * len(outs),
        scratch_shapes=scratch,
        compiler_params=pltpu.CompilerParams(vmem_limit_bytes=40 * 1024 * 1024),
        cost_estimate=pl.CostEstimate(flops=flops, bytes_accessed=nbytes, transcendentals=0),
    )


def routed_rows(picked_ref, held_ref):
    held = held_ref[...]
    chosen = [picked_ref[s : s + 1, :] == held for s in range(4)]
    routed = chosen[0] | chosen[1] | chosen[2] | chosen[3]
    routed_f = jnp.where(routed, 1.0, 0.0)
    before = lax.broadcasted_iota(jnp.int32, (TOK, TOK), 0) <= lax.broadcasted_iota(
        jnp.int32, (TOK, TOK), 1
    )
    upper = jnp.where(before, 1.0, 0.0).astype(BF)
    rank = dot(routed_f.astype(BF), upper, ((1,), (0,))) - 1.0
    slot = lax.broadcasted_iota(jnp.int32, (ROWS, TOK), 0) % CAPP
    sent = routed & (rank == slot.astype(F32))
    return chosen, sent


def dispatch_kernel(picked_ref, held_ref, gate_ref, place_ref, x_ref, g_ref, out_ref):
    chosen, sent = routed_rows(picked_ref, held_ref)
    sent_bf = jnp.where(sent, 1.0, 0.0).astype(BF)
    gate = jnp.zeros((ROWS, TOK), F32)
    for s in range(4):
        gate = gate + jnp.where(chosen[s] & sent, gate_ref[s : s + 1, :], 0.0)
    gate = jnp.sum(gate, axis=1, keepdims=True)
    rows = dot(sent_bf, x_ref[...], ((1,), (0,))).astype(BF)
    feature = lax.broadcasted_iota(jnp.int32, (D, 256), 0)
    for c in range(DP // 256):
        pick = jnp.where(feature == place_ref[:, c * 256 : (c + 1) * 256], 1.0, 0.0).astype(BF)
        out_ref[:, c * 256 : (c + 1) * 256] = dot(rows, pick, ((1,), (0,))).astype(BF)
    grads = dot(sent_bf, g_ref[...], ((1,), (0,))).astype(BF)
    out_ref[:, DP:] = jnp.concatenate(
        [grads, jnp.broadcast_to(gate, (ROWS, SEND - DP - F)).astype(BF)], axis=1
    )


def expert_kernel(got_ref, wm_ref, wo_ref, back_ref, pg_ref, pre_ref):
    step = 512
    for lo in range(0, F, step):
        hi = min(F, lo + step)
        pre_ref[:, lo:hi] = dot(got_ref[:, :HALF], wm_ref[:, lo:hi], ((1,), (0,))) + dot(
            got_ref[:, HALF:DP], wo_ref[:, lo:hi], ((1,), (0,))
        )
    gate = got_ref[:, DP + F : DP + F + 1].astype(F32)
    total = jnp.zeros((ROWS, 1), F32)
    for lo in range(0, F, step):
        hi = min(F, lo + step)
        pre = pre_ref[:, lo:hi]
        grad = got_ref[:, DP + lo : DP + hi].astype(F32)
        sig = 1.0 / (1.0 + jnp.exp(-pre))
        total = total + jnp.sum(grad * (pre * sig), axis=1, keepdims=True)
        slope = sig * (1.0 + pre * (1.0 - sig))
        pg_ref[:, lo:hi] = (gate * grad * slope).astype(BF)
    pg = pg_ref[...]
    for c in range(HALF // 256):
        r = slice(c * 256, (c + 1) * 256)
        back_ref[:, c * 256 : (c + 1) * 256] = dot(pg, wm_ref[r, :], ((1,), (1,))).astype(BF)
        back_ref[:, HALF + c * 256 : HALF + (c + 1) * 256] = dot(
            pg, wo_ref[r, :], ((1,), (1,))
        ).astype(BF)
    back_ref[:, DP:] = jnp.broadcast_to(total, (ROWS, BACK - DP)).astype(BF)


def attention_kernel(
    core_ref, picked_ref, held_ref, place_ref, back_ref, skip_ref, om_ref, oo_ref,
    q_ref, far_ref, near_ref, own_ref, label_ref,
    src_ref, gate_ref, qg_ref, farg_ref, nearg_ref, owng_ref,
    hidden_s, cot_s, kv_s, bias_s, acck_s, accv_s,
):
    chosen, sent = routed_rows(picked_ref, held_ref)
    sent_bf = jnp.where(sent, 1.0, 0.0).astype(BF)
    gate_part = back_ref[:, DP : DP + 1].astype(F32)
    for s in range(4):
        gate_ref[s : s + 1, :] = jnp.sum(
            jnp.where(chosen[s] & sent, gate_part, 0.0), axis=0, keepdims=True
        )
    src = dot(sent_bf, back_ref[:, :DP], ((0,), (0,))).astype(BF)
    feature = lax.broadcasted_iota(jnp.int32, (D, 256), 0)
    total = jnp.zeros((TOK, D), F32)
    for c in range(DP // 256):
        pick = jnp.where(feature == place_ref[:, c * 256 : (c + 1) * 256], 1.0, 0.0).astype(BF)
        total = total + dot(src[:, c * 256 : (c + 1) * 256], pick, ((1,), (1,)))
    src_ref[...] = total.astype(BF)
    hidden_s[...] = (skip_ref[...].astype(F32) + total).astype(BF)

    first = core_ref[0] == 0

    @pl.loop(0, 8)
    def _(z):
        base = pl.multiple_of(z * 128, 128)
        mine, other = om_ref[pl.ds(base, 128), :], oo_ref[pl.ds(base, 128), :]
        even, odd = jnp.where(first, mine, other), jnp.where(first, other, mine)
        rows = jnp.concatenate([even[:64], odd[:64], even[64:], odd[64:]], axis=0)
        cot_s[:, pl.ds(pl.multiple_of(z * 256, 256), 256)] = dot(
            hidden_s[...], rows, ((1,), (1,))
        ).astype(BF)

    for part, ref in enumerate((far_ref, near_ref, own_ref)):
        kv_s[part * TOK : (part + 1) * TOK, :] = ref[...]
    marks = kv_s[:, 2 * KV :].astype(F32)
    docs = marks[:, 0:1] * 16.0 + marks[:, 1:2]
    r_at = lax.broadcasted_iota(jnp.int32, (3 * TOK, TOK), 0)
    p_at = lax.broadcasted_iota(jnp.int32, (3 * TOK, TOK), 1)
    allowed = (r_at <= 2 * TOK + p_at) & (docs == label_ref[...])
    bias = jnp.where(allowed, 0.0, -1e30)
    bias_s[...] = jnp.concatenate([bias, bias], axis=1)

    low = lax.broadcasted_iota(jnp.int32, (TOK, 128), 1) < HD
    low_win = lax.broadcasted_iota(jnp.int32, (3 * TOK, 128), 1) < HD
    sums = []
    for g in range(KV_HEADS):
        k_one = kv_s[:, g * HD : (g + 1) * HD]
        v_one = kv_s[:, KV + g * HD : KV + (g + 1) * HD]
        k_two = jnp.concatenate([k_one, k_one], axis=1)
        v_two = jnp.concatenate([v_one, v_one], axis=1)
        k_flip = jnp.transpose(k_two.astype(F32))[:HD].astype(BF)
        acck_s[...] = jnp.zeros_like(acck_s)
        accv_s[...] = jnp.zeros_like(accv_s)

        def pair(i, carry, g=g, k_two=k_two, v_two=v_two, k_flip=k_flip):
            at = pl.ds(pl.multiple_of((g * 4 + i) * 128, 128), 128)
            q = q_ref[:, at] * 0.125
            c = cot_s[:, at]
            zero = jnp.zeros_like(q)
            q_st = jnp.concatenate([jnp.where(low, q, zero), jnp.where(low, zero, q)], axis=0)
            c_st = jnp.concatenate([jnp.where(low, c, zero), jnp.where(low, zero, c)], axis=0)
            s = dot(k_two, q_st, ((1,), (1,))) + bias_s[...]
            e = jnp.exp(s - jnp.max(s, axis=0, keepdims=True))
            shares = e * (1.0 / jnp.sum(e, axis=0, keepdims=True))
            shares_low = shares.astype(BF)
            dp = dot(v_two, c_st, ((1,), (1,)))
            centre = jnp.sum(shares_low.astype(F32) * dp, axis=0, keepdims=True)
            sg = (shares * (dp - centre)).astype(BF)
            acck_s[...] += dot(sg, q_st, ((1,), (0,)))
            accv_s[...] += dot(shares_low, c_st, ((1,), (0,)))
            qg = dot(k_flip, sg, ((1,), (0,)))
            both = jnp.concatenate([qg[:, :TOK], qg[:, TOK:]], axis=0) * 0.125
            qg_ref[:, at] = jnp.transpose(both).astype(BF)
            return carry

        lax.fori_loop(0, 4, pair, 0)
        ak, av = acck_s[...], accv_s[...]
        sums.append((ak + pltpu.roll(ak, HD, 1), av + pltpu.roll(av, HD, 1)))
    for kind in range(2):
        for t in range(2):
            tile = jnp.where(low_win, sums[2 * t][kind], sums[2 * t + 1][kind])
            at = slice(kind * KV + t * 128, kind * KV + (t + 1) * 128)
            farg_ref[:, at] = tile[:TOK].astype(BF)
            nearg_ref[:, at] = tile[TOK : 2 * TOK].astype(BF)
            owng_ref[:, at] = tile[2 * TOK :]


def gather_ring(pair):
    rows = pair.shape[0]
    half = rows // 2
    z = lax.axis_index("z")
    up = [(i, (i + 1) % 8) for i in range(8)]
    down = [(i, (i + 7) % 8) for i in range(8)]
    full = jnp.zeros((8 * rows,) + pair.shape[1:], pair.dtype)

    def put(full, piece, at, shift=0):
        return lax.dynamic_update_slice_in_dim(full, piece, (at % 8) * rows + shift, 0)

    full = put(full, pair, z)
    left = right = pair
    for k in range(1, 4):
        right = lax.ppermute(right, "z", up)
        left = lax.ppermute(left, "z", down)
        full = put(full, right, z - k + 8)
        full = put(full, left, z + k)
    last_r = lax.ppermute(right[:half], "z", up)
    last_l = lax.ppermute(left[half:], "z", down)
    full = put(full, last_r, z + 4)
    return put(full, last_l, z + 4, half)


def both_xh(piece):
    got = lax.ppermute(piece, "xh", SWAP)
    first = lax.axis_index("xh") == 0
    return jnp.concatenate([jnp.where(first, piece, got), jnp.where(first, got, piece)], axis=0)


def shift_blocks(value, steps):
    first, last = max(0, -steps), min(512, 512 - steps)
    return lax.ppermute(value, ALL, [(i, i + steps) for i in range(first, last)])


def shards(q, keys, values, label, skip, x, g, picked, mix, retained, weights, out_map):
    core = lax.axis_index("core")
    w_pair = both_xh(jnp.pad(weights[0], ((0, SEG - SHARD), (0, 0))))
    o_pair = both_xh(out_map)
    plus = (label + 1).astype(jnp.int32)
    marks = jnp.stack([plus // 16, plus % 16], axis=1).astype(BF)
    own = jnp.concatenate(
        [keys, values, jnp.pad(marks, ((0, 0), (0, WIDE - 2 * KV - 2)))], axis=1
    )
    near = shift_blocks(own, 1)
    far = shift_blocks(own, 2)

    o_mine = lax.all_gather(o_pair, "z", axis=0, tiled=True)

    picked_t = picked.T
    held = jnp.repeat(retained[:EXPERTS], CAPP)[:, None]
    spot = jnp.arange(DP, dtype=jnp.int32)
    half = spot // HALF
    rest = spot % HALF
    within = rest % SEG
    owner = (rest // SEG) * 2 + (half ^ core)
    place = jnp.where(within < SHARD, owner * SHARD + within, -1)[None, :]
    send = call(
        dispatch_kernel,
        [jax.ShapeDtypeStruct((ROWS, SEND), BF)],
        [],
        2 * TOK * D * (DP + 256),
        3 << 20,
        0,
        6,
    )(picked_t, held, mix.astype(F32).T, place, x, g)[0]
    got = lax.all_to_all(send.reshape(EXPERTS, CAPP, SEND), CTX, 0, 0, tiled=True)
    got = got.reshape(ROWS, SEND)

    w_mine = gather_ring(w_pair)
    w_other = lax.ppermute(w_mine, "core", SWAP)
    o_other = lax.ppermute(o_mine, "core", SWAP)

    x_swapped = lax.ppermute(got[:, HALF:DP], "core", SWAP)
    back, pg = call(
        expert_kernel,
        [jax.ShapeDtypeStruct((ROWS, BACK), BF), jax.ShapeDtypeStruct((ROWS, F), BF)],
        [pltpu.VMEM((ROWS, F), F32)],
        4 * ROWS * DP * F,
        6 << 20,
        0,
        3,
    )(got, w_mine, w_other)
    returned = lax.all_to_all(back.reshape(EXPERTS, CAPP, BACK), CTX, 0, 0, tiled=True)
    returned = returned.reshape(ROWS, BACK)

    pg_swapped = lax.ppermute(pg, "core", SWAP)
    x_rows = jnp.concatenate([got[:, :HALF], x_swapped], axis=0)
    pg_rows = jnp.concatenate([pg, pg_swapped], axis=0)
    partial = dot(x_rows, pg_rows, ((0,), (0,))).astype(BF)
    terms = lax.all_to_all(partial.reshape(16, SEG, F), ("z", "xh"), 0, 0, tiled=True)
    map_grad = jnp.sum(terms.astype(F32), axis=0).astype(BF)[None, :SHARD]

    src, gate_t, q_grad, far_g, near_g, own_g = call(
        attention_kernel,
        [
            jax.ShapeDtypeStruct((TOK, D), BF),
            jax.ShapeDtypeStruct((4, TOK), F32),
            jax.ShapeDtypeStruct((TOK, HEADS * HD), BF),
            jax.ShapeDtypeStruct((TOK, 2 * KV), BF),
            jax.ShapeDtypeStruct((TOK, 2 * KV), BF),
            jax.ShapeDtypeStruct((TOK, 2 * KV), F32),
        ],
        [
            pltpu.VMEM((TOK, D), BF),
            pltpu.VMEM((TOK, HEADS * HD), BF),
            pltpu.VMEM((3 * TOK, WIDE), BF),
            pltpu.VMEM((3 * TOK, 2 * TOK), F32),
            pltpu.VMEM((3 * TOK, 128), F32),
            pltpu.VMEM((3 * TOK, 128), F32),
        ],
        3 << 30,
        9 << 20,
        1,
        12,
    )(
        core[None].astype(jnp.int32), picked_t, held, place, returned, skip, o_mine, o_other,
        q, far, near, own, plus.astype(F32)[None, :],
    )
    got_near = shift_blocks(near_g, -1)
    got_far = shift_blocks(far_g, -2)
    kv_grad = (own_g + got_near.astype(F32) + got_far.astype(F32)).astype(BF)
    return (
        q_grad,
        kv_grad[:, :KV],
        kv_grad[:, KV:],
        src,
        gate_t.T.astype(BF),
        map_grad,
    )


def solution(mesh):
    fine = Mesh(mesh.devices.reshape(8, 2, 8, 2, 2), ALL)
    rows = P(ALL, None)
    fsdp = ("z", "xh", "core")
    return jax.shard_map(
        shards,
        mesh=fine,
        in_specs=(
            rows, rows, rows, P(ALL), rows, rows, rows, rows, rows, P(),
            P(CTX, fsdp, None), P(fsdp, None),
        ),
        out_specs=(rows, rows, rows, rows, rows, P(CTX, fsdp, None)),
        check_vma=False,
    )
```

```python
import jax
import jax.numpy as jnp
from jax import lax
from jax.experimental import pallas as pl
from jax.experimental.pallas import tpu as pltpu
from jax.sharding import Mesh, PartitionSpec as P

TOK = 128
D = 1440
F = 1440
HEADS = 32
KV_HEADS = 4
HD = 64
CAP = 6
CAPP = 8
EXPERTS = 16
ROWS = EXPERTS * CAPP
SEG = 48
SHARD = 45
DP = 1536
HALF = 768
SEND = 3072
BACK = 1664
KV = 256
WIDE = 640
BF = jnp.bfloat16
F32 = jnp.float32
ALL = ("y", "xl", "z", "xh", "core")
CTX = ("y", "xl")
SWAP = ((0, 1), (1, 0))


def dot(a, b, dims):
    return lax.dot_general(a, b, (dims, ((), ())), preferred_element_type=F32)


def spec_vmem():
    return pl.BlockSpec(memory_space=pltpu.VMEM)


def spec_smem():
    return pl.BlockSpec(memory_space=pltpu.SMEM)


def out(shape, dtype=BF):
    return jax.ShapeDtypeStruct(shape, dtype)


def call(kernel, outs, scratch, weight_us, n_smem, n_vmem, n_any=0):
    return pl.pallas_call(
        kernel,
        out_shape=outs,
        in_specs=[spec_smem()] * n_smem
        + [spec_vmem()] * n_vmem
        + [pl.BlockSpec(memory_space=pl.ANY)] * n_any,
        out_specs=[spec_vmem()] * len(outs),
        scratch_shapes=scratch,
        compiler_params=pltpu.CompilerParams(vmem_limit_bytes=26 * 1024 * 1024),
        cost_estimate=pl.CostEstimate(
            flops=0, bytes_accessed=int(weight_us * 3690000), transcendentals=0
        ),
    )


def order(value, *ties):
    return lax.optimization_barrier((value, *ties))[0]


def dispatch_kernel(picked_ref, held_ref, gate_ref, place_ref, x_ref, g_ref, out_ref, sent_ref):
    held = held_ref[...]
    chosen = [picked_ref[s : s + 1, :] == held for s in range(4)]
    routed = chosen[0] | chosen[1] | chosen[2] | chosen[3]
    routed_f = jnp.where(routed, 1.0, 0.0)
    before = lax.broadcasted_iota(jnp.int32, (TOK, TOK), 0) <= lax.broadcasted_iota(
        jnp.int32, (TOK, TOK), 1
    )
    upper = jnp.where(before, 1.0, 0.0).astype(BF)
    rank = dot(routed_f.astype(BF), upper, ((1,), (0,))) - 1.0
    slot = lax.broadcasted_iota(jnp.int32, (ROWS, TOK), 0) % CAPP
    sent = routed & (rank == slot.astype(F32))
    sent_bf = jnp.where(sent, 1.0, 0.0).astype(BF)
    sent_ref[...] = sent_bf
    gate = jnp.zeros((ROWS, TOK), F32)
    for s in range(4):
        gate = gate + jnp.where(chosen[s] & sent, gate_ref[s : s + 1, :], 0.0)
    gate = jnp.sum(gate, axis=1, keepdims=True)
    rows = dot(sent_bf, x_ref[...], ((1,), (1,))).astype(BF)
    feature = lax.broadcasted_iota(jnp.int32, (D, 256), 0)
    for c in range(DP // 256):
        pick = jnp.where(feature == place_ref[:, c * 256 : (c + 1) * 256], 1.0, 0.0).astype(BF)
        out_ref[:, c * 256 : (c + 1) * 256] = dot(rows, pick, ((1,), (0,))).astype(BF)
    grads = dot(sent_bf, g_ref[...], ((1,), (1,))).astype(BF)
    out_ref[:, DP:] = jnp.concatenate(
        [grads, jnp.broadcast_to(gate, (ROWS, SEND - DP - F)).astype(BF)], axis=1
    )


def shares_kernel(q_ref, far_ref, near_ref, own_ref, label_ref, shares_ref, qt_ref, kt_ref, v_ref, kv_s, bias_s):
    for part, ref in enumerate((far_ref, near_ref, own_ref)):
        kv_s[part * TOK : (part + 1) * TOK, :] = ref[...]
    marks = kv_s[:, 2 * KV :].astype(F32)
    docs = marks[:, 0:1] * 16.0 + marks[:, 1:2]
    r_at = lax.broadcasted_iota(jnp.int32, (3 * TOK, TOK), 0)
    p_at = lax.broadcasted_iota(jnp.int32, (3 * TOK, TOK), 1)
    allowed = (r_at <= 2 * TOK + p_at) & (docs == label_ref[...])
    bias = jnp.where(allowed, 0.0, -1e30)
    bias_s[...] = jnp.concatenate([bias, bias], axis=1)
    v_ref[...] = kv_s[:, KV : 2 * KV]
    for t in range(2):
        kt_ref[t * 128 : (t + 1) * 128, :] = jnp.transpose(
            kv_s[:, t * 128 : (t + 1) * 128].astype(F32)
        ).astype(BF)
    for g in range(KV_HEADS):
        k_one = kv_s[:, g * HD : (g + 1) * HD]

        def pair(i, carry, g=g, k_one=k_one):
            at = pl.multiple_of((g * 4 + i) * 128, 128)
            flipped = jnp.transpose(q_ref[:, pl.ds(at, 128)].astype(F32) * 0.125).astype(BF)
            qt_ref[pl.ds(at, 128), :] = flipped
            q_two = jnp.concatenate([flipped[:HD], flipped[HD:]], axis=1)
            s = dot(k_one, q_two, ((1,), (0,))) + bias_s[...]
            e = jnp.exp(s - jnp.max(s, axis=0, keepdims=True))
            shares = e * (1.0 / jnp.sum(e, axis=0, keepdims=True))
            shares_ref[:, pl.ds(pl.multiple_of(2 * at, 256), 256)] = shares.astype(BF)
            return carry

        lax.fori_loop(0, 4, pair, 0)


def expert_kernel(got_ref, wm_ref, wo_ref, back_ref, pg_ref, pre_ref):
    step = 512
    for lo in range(0, DP, step):
        at = slice(lo, lo + step)
        pre_ref[:, at] = dot(got_ref[:, :HALF], wm_ref[:, at], ((1,), (0,))) + dot(
            got_ref[:, HALF:DP], wo_ref[:, at], ((1,), (0,))
        )
    gate = got_ref[:, DP + F : DP + F + 1].astype(F32)
    total = jnp.zeros((ROWS, 1), F32)
    for lo in range(0, DP, step):
        pre = pre_ref[:, lo : lo + step]
        grad = got_ref[:, DP + lo : DP + lo + step].astype(F32)
        sig = 1.0 / (1.0 + jnp.exp(-pre))
        total = total + jnp.sum(grad * (pre * sig), axis=1, keepdims=True)
        slope = sig * (1.0 + pre * (1.0 - sig))
        pg_ref[:, lo : lo + step] = (gate * grad * slope).astype(BF)
    pg = pg_ref[...]
    for c in range(HALF // 256):
        r = slice(c * 256, (c + 1) * 256)
        back_ref[:, c * 256 : (c + 1) * 256] = dot(pg, wm_ref[r, :], ((1,), (1,))).astype(BF)
        back_ref[:, HALF + c * 256 : HALF + (c + 1) * 256] = dot(
            pg, wo_ref[r, :], ((1,), (1,))
        ).astype(BF)
    back_ref[:, DP:] = jnp.broadcast_to(total, (ROWS, BACK - DP)).astype(BF)


def map_kernel(x_ref, x2_ref, pg_ref, pg2_ref, out_ref):
    pg = jnp.concatenate([pg_ref[...], pg2_ref[...]], axis=0)
    for c in range(HALF // 256):
        at = slice(c * 256, (c + 1) * 256)
        rows = jnp.concatenate([x_ref[:, at], x2_ref[:, at]], axis=0)
        out_ref[at, :] = dot(rows, pg, ((0,), (0,))).astype(BF)


def late_kernel(
    core_ref, picked_ref, held_ref, sent_ref, place_ref, back_ref, v_ref,
    skip_any, om_any, oo_any, qt_any, shares_any,
    src_ref, gate_ref, sg_ref, farg_ref, nearg_ref, owng_ref,
    hidden_s, cot_s, acck_s, accv_s, skip_ref, om_ref, oo_ref, qt_ref, shares_ref, sems,
):
    pairs = (
        (skip_any, skip_ref), (om_any, om_ref), (oo_any, oo_ref),
        (qt_any, qt_ref), (shares_any, shares_ref),
    )
    copies = [
        pltpu.make_async_copy(source, target, sems.at[i])
        for i, (source, target) in enumerate(pairs)
    ]
    for copy in copies:
        copy.start()
    sent_bf = sent_ref[...]
    sent = sent_bf.astype(F32) > 0.5
    held = held_ref[...]
    gate_part = back_ref[:, DP : DP + 1].astype(F32)
    for s in range(4):
        mine = (picked_ref[s : s + 1, :] == held) & sent
        gate_ref[s : s + 1, :] = jnp.sum(jnp.where(mine, gate_part, 0.0), axis=0, keepdims=True)
    src = dot(sent_bf, back_ref[:, :DP], ((0,), (0,))).astype(BF)
    feature = lax.broadcasted_iota(jnp.int32, (D, 256), 0)
    total = jnp.zeros((D, TOK), F32)
    for c in range(DP // 256):
        pick = jnp.where(feature == place_ref[:, c * 256 : (c + 1) * 256], 1.0, 0.0).astype(BF)
        total = total + dot(pick, src[:, c * 256 : (c + 1) * 256], ((1,), (1,)))
    src_ref[...] = total.astype(BF)
    copies[0].wait()
    hidden_s[:D, :] = (skip_ref[...].astype(F32) + total).astype(BF)
    hidden_s[D:, :] = jnp.zeros((DP - D, TOK), BF)

    core = core_ref[0]
    for ref, place, copy in (
        (om_ref, core * HD, copies[1]),
        (oo_ref, HD - core * HD, copies[2]),
    ):
        copy.wait()
        for c in range(4):
            block = dot(ref[c * 256 : (c + 1) * 256, :], hidden_s[...], ((1,), (0,))).astype(BF)
            for j in range(4):
                at = pl.multiple_of((c * 4 + j) * 128 + place, HD)
                cot_s[pl.ds(at, HD), :] = block[j * HD : (j + 1) * HD]

    copies[3].wait()
    copies[4].wait()
    for t in range(2):
        sums = []
        for g in (2 * t, 2 * t + 1):
            v_one = v_ref[:, g * HD : (g + 1) * HD]
            for i in range(4):
                n = g * 4 + i
                rows = slice(n * 128, n * 128 + HD), slice(n * 128 + HD, (n + 1) * 128)
                q_two = jnp.concatenate([qt_ref[rows[0], :], qt_ref[rows[1], :]], axis=1)
                c_two = jnp.concatenate([cot_s[rows[0], :], cot_s[rows[1], :]], axis=1)
                low = shares_ref[:, n * 256 : (n + 1) * 256]
                dp = dot(v_one, c_two, ((1,), (0,)))
                shares = low.astype(F32)
                centre = jnp.sum(shares * dp, axis=0, keepdims=True)
                sg = (shares * (dp - centre)).astype(BF)
                sg_ref[:, n * 256 : (n + 1) * 256] = sg
                ak = dot(sg, q_two, ((1,), (1,)))
                av = dot(low, c_two, ((1,), (1,)))
                if i == 0:
                    acck_s[...] = ak
                    accv_s[...] = av
                else:
                    acck_s[...] += ak
                    accv_s[...] += av
            sums.append((acck_s[...], accv_s[...]))
        for kind in range(2):
            tile = jnp.concatenate([sums[0][kind], sums[1][kind]], axis=1)
            at = slice(kind * KV + t * 128, kind * KV + (t + 1) * 128)
            farg_ref[:, at] = tile[:TOK].astype(BF)
            nearg_ref[:, at] = tile[TOK : 2 * TOK].astype(BF)
            owng_ref[:, at] = tile[2 * TOK :]


def query_kernel(sg_ref, kt_ref, qg_ref):
    for n in range(16):
        g = n // 4
        qg = dot(kt_ref[g * HD : (g + 1) * HD, :], sg_ref[:, n * 256 : (n + 1) * 256], ((1,), (0,)))
        both = jnp.concatenate([qg[:, :TOK], qg[:, TOK:]], axis=0) * 0.125
        qg_ref[:, n * 128 : (n + 1) * 128] = jnp.transpose(both).astype(BF)


RIGHT = [(i, (i + 1) % 8) for i in range(8)]
LEFT = [(i, (i + 7) % 8) for i in range(8)]


def reduce_start(parts, returned):
    half = parts.shape[1] // 2
    z = lax.axis_index("z")

    def chunk(k):
        return lax.dynamic_index_in_dim(parts, (z + k) % 8, 0, keepdims=False)

    right = lax.ppermute(chunk(4)[:half], "z", RIGHT)
    left = lax.ppermute(chunk(4)[half:], "z", LEFT)
    right, left = lax.optimization_barrier((right, left))
    right = jnp.pad(right, ((0, half), (0, 0)))
    left = jnp.pad(left, ((half, 0), (0, 0)))
    for k in (3, 2):
        right = (chunk(k).astype(F32) + right.astype(F32)).astype(BF)
        left = (chunk(8 - k).astype(F32) + left.astype(F32)).astype(BF)
        ties = (returned,) if k == 2 else ()
        right, left = lax.optimization_barrier((right, left, *ties))[:2]
        right = lax.ppermute(right, "z", RIGHT)
        left = lax.ppermute(left, "z", LEFT)
        right, left = lax.optimization_barrier((right, left))
    right = (chunk(1).astype(F32) + right.astype(F32)).astype(BF)
    left = (chunk(7).astype(F32) + left.astype(F32)).astype(BF)
    return right, left, chunk(0)


def reduce_end(right, left, mine, late):
    right, left = lax.optimization_barrier((right, left, late))[:2]
    right = lax.ppermute(right, "z", RIGHT)
    left = lax.ppermute(left, "z", LEFT)
    return mine.astype(F32) + right.astype(F32) + left.astype(F32)


def both_xh(piece):
    other = lax.ppermute(piece, "xh", SWAP)
    lower = lax.axis_index("xh") == 0
    return jnp.concatenate(
        [jnp.where(lower, piece, other), jnp.where(lower, other, piece)], axis=0
    )


def shift_blocks(value, steps):
    first, last = max(0, -steps), min(512, 512 - steps)
    return lax.ppermute(value, ALL, [(i, i + steps) for i in range(first, last)])


def shards(q, keys, values, label, skip, x, g, picked, mix, retained, weights, out_map):
    core = lax.axis_index("core")
    w_pad = jnp.pad(weights[0], ((0, SEG - SHARD), (0, DP - F)))
    o_pad = jnp.pad(out_map, ((0, 0), (0, DP - D)))
    w_pair = both_xh(w_pad)
    w_mine = lax.all_gather(w_pair, "z", axis=0, tiled=True)

    plus = (label + 1).astype(jnp.int32)
    marks = jnp.stack([plus // 16, plus % 16], axis=1).astype(BF)
    own = jnp.concatenate(
        [keys, values, jnp.pad(marks, ((0, 0), (0, WIDE - 2 * KV - 2)))], axis=1
    )
    picked_t = order(picked.T, w_pair)
    held = jnp.repeat(retained[:EXPERTS], CAPP)[:, None]
    spot = jnp.arange(DP, dtype=jnp.int32)
    half = spot // HALF
    rest = spot % HALF
    within = rest % SEG
    owner = (rest // SEG) * 2 + (half ^ core)
    place = jnp.where(within < SHARD, owner * SHARD + within, -1)[None, :]
    send, sent = call(dispatch_kernel, [out((ROWS, SEND)), out((ROWS, TOK))], [], 2, 0, 6)(
        picked_t, held, mix.astype(F32).T, place, x.T, g.T
    )
    o_pair = both_xh(order(o_pad, send))
    o_mine = lax.all_gather(o_pair, "z", axis=0, tiled=True)
    got = lax.all_to_all(send.reshape(EXPERTS, CAPP, SEND), CTX, 0, 0, tiled=True)
    got = got.reshape(ROWS, SEND)
    x_swapped = lax.ppermute(got[:, HALF:DP], "core", SWAP)
    own = order(own, send)
    near = shift_blocks(own, 1)
    far = shift_blocks(own, 2)

    shares, q_t, k_t, v_win = call(
        shares_kernel,
        [
            out((3 * TOK, HEADS * TOK)),
            out((HEADS * HD, TOK)),
            out((KV, 3 * TOK)),
            out((3 * TOK, KV)),
        ],
        [pltpu.VMEM((3 * TOK, WIDE), BF), pltpu.VMEM((3 * TOK, 2 * TOK), F32)],
        8,
        0,
        5,
    )(q, far, near, own, plus.astype(F32)[None, :])

    w_mine = order(w_mine, v_win, x_swapped, o_pair)
    w_other = lax.ppermute(w_mine, "core", SWAP)
    back, pg = call(
        expert_kernel,
        [out((ROWS, BACK)), out((ROWS, DP))],
        [pltpu.VMEM((ROWS, DP), F32)],
        3,
        0,
        3,
    )(got, w_mine, w_other)
    returned = lax.all_to_all(back.reshape(EXPERTS, CAPP, BACK), CTX, 0, 0, tiled=True)
    returned = returned.reshape(ROWS, BACK)

    pg_swapped = lax.ppermute(pg, "core", SWAP)
    partial = call(map_kernel, [out((HALF, DP))], [], 2, 0, 4)(
        got[:, :HALF], x_swapped, pg, pg_swapped
    )[0]
    right, left, mine = reduce_start(partial.reshape(8, 2 * SEG, DP), returned)
    o_mine = order(o_mine, right, left)
    o_other = lax.ppermute(o_mine, "core", SWAP)
    src_t, gate_t, sg, far_g, near_g, own_g = call(
        late_kernel,
        [
            out((D, TOK)),
            out((4, TOK), F32),
            out((3 * TOK, HEADS * TOK)),
            out((TOK, 2 * KV)),
            out((TOK, 2 * KV)),
            out((TOK, 2 * KV), F32),
        ],
        [
            pltpu.VMEM((DP, TOK), BF),
            pltpu.VMEM((HEADS * HD, TOK), BF),
            pltpu.VMEM((3 * TOK, HD), F32),
            pltpu.VMEM((3 * TOK, HD), F32),
            pltpu.VMEM((D, TOK), BF),
            pltpu.VMEM((16 * HD, DP), BF),
            pltpu.VMEM((16 * HD, DP), BF),
            pltpu.VMEM((HEADS * HD, TOK), BF),
            pltpu.VMEM((3 * TOK, HEADS * TOK), BF),
            pltpu.SemaphoreType.DMA((5,)),
        ],
        8,
        1,
        6,
        5,
    )(
        core[None].astype(jnp.int32), picked_t, held, sent, place, returned, v_win,
        skip.T, o_mine, o_other, q_t, shares,
    )
    merged = reduce_end(right, left, mine, near_g)
    xh = lax.axis_index("xh")
    away = lax.dynamic_slice_in_dim(merged, (1 - xh) * SEG, SEG, 0).astype(BF)
    kept = lax.dynamic_slice_in_dim(merged, xh * SEG, SEG, 0)
    map_grad = (kept + lax.ppermute(away, "xh", SWAP).astype(F32)).astype(BF)
    map_grad = map_grad[None, :SHARD, :F]

    got_near = shift_blocks(near_g, -1)
    got_far = shift_blocks(far_g, -2)
    q_grad = call(query_kernel, [out((TOK, HEADS * HD))], [], 3, 0, 2)(sg, k_t)[0]
    kv_grad = (own_g + got_near.astype(F32) + got_far.astype(F32)).astype(BF)
    return (
        q_grad,
        kv_grad[:, :KV],
        kv_grad[:, KV:],
        src_t.T,
        gate_t.T.astype(BF),
        map_grad,
    )


def solution(mesh):
    fine = Mesh(mesh.devices.reshape(8, 2, 8, 2, 2), ALL)
    rows = P(ALL, None)
    fsdp = ("z", "xh", "core")
    return jax.shard_map(
        shards,
        mesh=fine,
        in_specs=(
            rows, rows, rows, P(ALL), rows, rows, rows, rows, rows, P(),
            P(CTX, fsdp, None), P(fsdp, None),
        ),
        out_specs=(rows, rows, rows, rows, rows, P(CTX, fsdp, None)),
        check_vma=False,
    )
```

```python
import jax
import jax.numpy as jnp
from jax import lax
from jax.experimental import pallas as pl
from jax.experimental.pallas import tpu as pltpu
from jax.sharding import Mesh, PartitionSpec as P

TOK = 128
D = 1440
F = 1440
HEADS = 32
KV_HEADS = 4
HD = 64
CAP = 6
CAPP = 8
EXPERTS = 16
ROWS = EXPERTS * CAPP
SEG = 48
SHARD = 45
DP = 1536
HALF = 768
SEND = 3072
BACK = 1664
KV = 256
WIDE = 640
BF = jnp.bfloat16
F32 = jnp.float32
ALL = ("y", "xl", "z", "xh", "core")
CTX = ("y", "xl")
SWAP = ((0, 1), (1, 0))


def dot(a, b, dims):
    return lax.dot_general(a, b, (dims, ((), ())), preferred_element_type=F32)


SPACES = {"s": pltpu.SMEM, "v": pltpu.VMEM, "h": pltpu.HBM}


def out(shape, dtype=BF):
    return jax.ShapeDtypeStruct(shape, dtype)


def call(kernel, ins, outs, out_spaces, scratch, weight_us):
    return pl.pallas_call(
        kernel,
        out_shape=outs,
        in_specs=[pl.BlockSpec(memory_space=SPACES[k]) for k in ins],
        out_specs=[pl.BlockSpec(memory_space=SPACES[k]) for k in out_spaces],
        scratch_shapes=scratch,
        compiler_params=pltpu.CompilerParams(vmem_limit_bytes=60 * 1024 * 1024),
        cost_estimate=pl.CostEstimate(
            flops=0, bytes_accessed=int(weight_us * 3690000), transcendentals=0
        ),
    )


def copies_of(pairs, sems):
    return [pltpu.make_async_copy(a, b, sems.at[i]) for i, (a, b) in enumerate(pairs)]


def order(value, *ties):
    return lax.optimization_barrier((value, *ties))[0]


def dispatch_kernel(
    picked_ref, held_ref, gate_ref, place_ref, x_ref, g_ref, out_ref, sent_any, sent_ref, sems
):
    held = held_ref[...]
    chosen = [picked_ref[s : s + 1, :] == held for s in range(4)]
    routed = chosen[0] | chosen[1] | chosen[2] | chosen[3]
    routed_f = jnp.where(routed, 1.0, 0.0)
    before = lax.broadcasted_iota(jnp.int32, (TOK, TOK), 0) <= lax.broadcasted_iota(
        jnp.int32, (TOK, TOK), 1
    )
    upper = jnp.where(before, 1.0, 0.0).astype(BF)
    rank = dot(routed_f.astype(BF), upper, ((1,), (0,))) - 1.0
    slot = lax.broadcasted_iota(jnp.int32, (ROWS, TOK), 0) % CAPP
    sent = routed & (rank == slot.astype(F32))
    sent_bf = jnp.where(sent, 1.0, 0.0).astype(BF)
    sent_ref[...] = sent_bf
    copy = pltpu.make_async_copy(sent_ref, sent_any, sems.at[0])
    copy.start()
    gate = jnp.zeros((ROWS, TOK), F32)
    for s in range(4):
        gate = gate + jnp.where(chosen[s] & sent, gate_ref[s : s + 1, :], 0.0)
    gate = jnp.sum(gate, axis=1, keepdims=True)
    rows = dot(sent_bf, x_ref[...], ((1,), (1,))).astype(BF)
    feature = lax.broadcasted_iota(jnp.int32, (D, 256), 0)
    for c in range(DP // 256):
        pick = jnp.where(feature == place_ref[:, c * 256 : (c + 1) * 256], 1.0, 0.0).astype(BF)
        out_ref[:, c * 256 : (c + 1) * 256] = dot(rows, pick, ((1,), (0,))).astype(BF)
    grads = dot(sent_bf, g_ref[...], ((1,), (1,))).astype(BF)
    out_ref[:, DP:] = jnp.concatenate(
        [grads, jnp.broadcast_to(gate, (ROWS, SEND - DP - F)).astype(BF)], axis=1
    )
    copy.wait()


def shares_kernel(
    q_ref, far_ref, near_ref, own_ref, label_ref, shares_any, qt_any, kt_any, v_any,
    kv_s, bias_s, shares_ref, qt_ref, kt_ref, v_ref, sems,
):
    for part, ref in enumerate((far_ref, near_ref, own_ref)):
        kv_s[part * TOK : (part + 1) * TOK, :] = ref[...]
    marks = kv_s[:, 2 * KV :].astype(F32)
    docs = marks[:, 0:1] * 16.0 + marks[:, 1:2]
    r_at = lax.broadcasted_iota(jnp.int32, (3 * TOK, TOK), 0)
    p_at = lax.broadcasted_iota(jnp.int32, (3 * TOK, TOK), 1)
    allowed = (r_at <= 2 * TOK + p_at) & (docs == label_ref[...])
    bias = jnp.where(allowed, 0.0, -1e30)
    bias_s[...] = jnp.concatenate([bias, bias], axis=1)
    v_ref[...] = kv_s[:, KV : 2 * KV]
    for t in range(2):
        kt_ref[t * 128 : (t + 1) * 128, :] = jnp.transpose(
            kv_s[:, t * 128 : (t + 1) * 128].astype(F32)
        ).astype(BF)
    copies = []
    for g in range(KV_HEADS):
        k_one = kv_s[:, g * HD : (g + 1) * HD]

        def pair(i, carry, g=g, k_one=k_one):
            at = pl.multiple_of((g * 4 + i) * 128, 128)
            flipped = jnp.transpose(q_ref[:, pl.ds(at, 128)].astype(F32) * 0.125).astype(BF)
            qt_ref[pl.ds(at, 128), :] = flipped
            q_two = jnp.concatenate([flipped[:HD], flipped[HD:]], axis=1)
            s = dot(k_one, q_two, ((1,), (0,))) + bias_s[...]
            e = jnp.exp(s - jnp.max(s, axis=0, keepdims=True))
            shares = e * (1.0 / jnp.sum(e, axis=0, keepdims=True))
            shares_ref[:, pl.ds(pl.multiple_of(2 * at, 256), 256)] = shares.astype(BF)
            return carry

        lax.fori_loop(0, 4, pair, 0)
        columns = slice(g * 8 * TOK, (g + 1) * 8 * TOK)
        copies.append(
            pltpu.make_async_copy(
                shares_ref.at[:, columns], shares_any.at[:, columns], sems.at[g]
            )
        )
        copies[-1].start()
    pairs = ((qt_ref, qt_any), (kt_ref, kt_any), (v_ref, v_any))
    for i, (source, target) in enumerate(pairs):
        copies.append(pltpu.make_async_copy(source, target, sems.at[4 + i]))
        copies[-1].start()
    for copy in copies:
        copy.wait()


def expert_kernel(
    got_ref, wm_any, wo_any, back_any, pg_any, wm_ref, wo_ref, back_ref, pg_ref, pre_ref, sems
):
    loads = copies_of(((wm_any, wm_ref), (wo_any, wo_ref)), sems)
    for copy in loads:
        copy.start()
    for copy in loads:
        copy.wait()
    step = 512
    for lo in range(0, DP, step):
        at = slice(lo, lo + step)
        pre_ref[:, at] = dot(got_ref[:, :HALF], wm_ref[:, at], ((1,), (0,))) + dot(
            got_ref[:, HALF:DP], wo_ref[:, at], ((1,), (0,))
        )
    gate = got_ref[:, DP + F : DP + F + 1].astype(F32)
    total = jnp.zeros((ROWS, 1), F32)
    for lo in range(0, DP, step):
        pre = pre_ref[:, lo : lo + step]
        grad = got_ref[:, DP + lo : DP + lo + step].astype(F32)
        sig = 1.0 / (1.0 + jnp.exp(-pre))
        total = total + jnp.sum(grad * (pre * sig), axis=1, keepdims=True)
        slope = sig * (1.0 + pre * (1.0 - sig))
        pg_ref[:, lo : lo + step] = (gate * grad * slope).astype(BF)
    store = pltpu.make_async_copy(pg_ref, pg_any, sems.at[2])
    store.start()
    pg = pg_ref[...]
    for c in range(HALF // 256):
        r = slice(c * 256, (c + 1) * 256)
        back_ref[:, c * 256 : (c + 1) * 256] = dot(pg, wm_ref[r, :], ((1,), (1,))).astype(BF)
        back_ref[:, HALF + c * 256 : HALF + (c + 1) * 256] = dot(
            pg, wo_ref[r, :], ((1,), (1,))
        ).astype(BF)
    back_ref[:, DP:] = jnp.broadcast_to(total, (ROWS, BACK - DP)).astype(BF)
    returned = pltpu.make_async_copy(back_ref, back_any, sems.at[3])
    returned.start()
    store.wait()
    returned.wait()


def map_kernel(
    x_any, x2_any, pg_any, pg2_any, out_ref, x_ref, x2_ref, pg_ref, pg2_ref, sems
):
    pairs = ((x_any, x_ref), (x2_any, x2_ref), (pg_any, pg_ref), (pg2_any, pg2_ref))
    loads = copies_of(pairs, sems)
    for copy in loads:
        copy.start()
    for copy in loads:
        copy.wait()
    pg = jnp.concatenate([pg_ref[...], pg2_ref[...]], axis=0)
    for c in range(HALF // 256):
        at = slice(c * 256, (c + 1) * 256)
        rows = jnp.concatenate([x_ref[:, at], x2_ref[:, at]], axis=0)
        out_ref[at, :] = dot(rows, pg, ((0,), (0,))).astype(BF)


def late_kernel(
    at_ref, picked_ref, held_ref, place_ref, back_ref,
    sent_any, v_any, skip_any, om_any, oo_any, qt_any, shares_any,
    src_ref, gate_ref, sg_ref, farg_ref, nearg_ref, owng_ref,
    hidden_s, cot_s, acck_s, accv_s,
    sent_ref, v_ref, skip_ref, om_ref, oo_ref, qt_ref, shares_ref, sems,
):
    pairs = (
        (sent_any, sent_ref), (skip_any, skip_ref), (om_any, om_ref), (oo_any, oo_ref),
        (v_any, v_ref), (qt_any, qt_ref), (shares_any, shares_ref),
    )
    copies = copies_of(pairs, sems)
    for copy in copies:
        copy.start()
    copies[0].wait()
    sent_bf = sent_ref[...]
    sent = sent_bf.astype(F32) > 0.5
    held = held_ref[...]
    gate_part = back_ref[:, DP : DP + 1].astype(F32)
    for s in range(4):
        mine = (picked_ref[s : s + 1, :] == held) & sent
        gate_ref[s : s + 1, :] = jnp.sum(jnp.where(mine, gate_part, 0.0), axis=0, keepdims=True)
    src = dot(sent_bf, back_ref[:, :DP], ((0,), (0,))).astype(BF)
    feature = lax.broadcasted_iota(jnp.int32, (D, 256), 0)
    total = jnp.zeros((D, TOK), F32)
    for c in range(DP // 256):
        pick = jnp.where(feature == place_ref[:, c * 256 : (c + 1) * 256], 1.0, 0.0).astype(BF)
        total = total + dot(pick, src[:, c * 256 : (c + 1) * 256], ((1,), (1,)))
    src_ref[...] = total.astype(BF)
    copies[1].wait()
    hidden_s[:D, :] = (skip_ref[...].astype(F32) + total).astype(BF)
    hidden_s[D:, :] = jnp.zeros((DP - D, TOK), BF)

    core, xh = at_ref[0], at_ref[1]
    for ref, place, copy in (
        (om_ref, core * HD, copies[2]),
        (oo_ref, HD - core * HD, copies[3]),
    ):
        copy.wait()
        for c in range(4):
            block = dot(ref[c * 256 : (c + 1) * 256, :], hidden_s[...], ((1,), (0,))).astype(BF)
            for j in range(4):
                across = xh if j % 2 == 0 else 1 - xh
                at = pl.multiple_of((c * 2 + j // 2) * 256 + across * 128 + place, HD)
                cot_s[pl.ds(at, HD), :] = block[j * HD : (j + 1) * HD]

    for copy in copies[4:]:
        copy.wait()
    for t in range(2):
        sums = []
        for g in (2 * t, 2 * t + 1):
            v_one = v_ref[:, g * HD : (g + 1) * HD]
            for i in range(4):
                n = g * 4 + i
                rows = slice(n * 128, n * 128 + HD), slice(n * 128 + HD, (n + 1) * 128)
                q_two = jnp.concatenate([qt_ref[rows[0], :], qt_ref[rows[1], :]], axis=1)
                c_two = jnp.concatenate([cot_s[rows[0], :], cot_s[rows[1], :]], axis=1)
                low = shares_ref[:, n * 256 : (n + 1) * 256]
                dp = dot(v_one, c_two, ((1,), (0,)))
                shares = low.astype(F32)
                centre = jnp.sum(shares * dp, axis=0, keepdims=True)
                sg = (shares * (dp - centre)).astype(BF)
                sg_ref[:, n * 256 : (n + 1) * 256] = sg
                ak = dot(sg, q_two, ((1,), (1,)))
                av = dot(low, c_two, ((1,), (1,)))
                if i == 0:
                    acck_s[...] = ak
                    accv_s[...] = av
                else:
                    acck_s[...] += ak
                    accv_s[...] += av
            sums.append((acck_s[...], accv_s[...]))
        for kind in range(2):
            tile = jnp.concatenate([sums[0][kind], sums[1][kind]], axis=1)
            at = slice(kind * KV + t * 128, kind * KV + (t + 1) * 128)
            farg_ref[:, at] = tile[:TOK].astype(BF)
            nearg_ref[:, at] = tile[TOK : 2 * TOK].astype(BF)
            owng_ref[:, at] = tile[2 * TOK :]


def query_kernel(sg_ref, kt_ref, qg_ref):
    for n in range(16):
        g = n // 4
        qg = dot(kt_ref[g * HD : (g + 1) * HD, :], sg_ref[:, n * 256 : (n + 1) * 256], ((1,), (0,)))
        both = jnp.concatenate([qg[:, :TOK], qg[:, TOK:]], axis=0) * 0.125
        qg_ref[:, n * 128 : (n + 1) * 128] = jnp.transpose(both).astype(BF)


RIGHT = [(i, (i + 1) % 8) for i in range(8)]
LEFT = [(i, (i + 7) % 8) for i in range(8)]


def reduce_start(parts, returned):
    half = parts.shape[1] // 2
    z = lax.axis_index("z")

    def chunk(k):
        return lax.dynamic_index_in_dim(parts, (z + k) % 8, 0, keepdims=False)

    right = lax.ppermute(chunk(4)[:half], "z", RIGHT)
    left = lax.ppermute(chunk(4)[half:], "z", LEFT)
    right, left = lax.optimization_barrier((right, left))
    right = jnp.pad(right, ((0, half), (0, 0)))
    left = jnp.pad(left, ((half, 0), (0, 0)))
    marks = []
    for k in (3, 2):
        right = (chunk(k).astype(F32) + right.astype(F32)).astype(BF)
        left = (chunk(8 - k).astype(F32) + left.astype(F32)).astype(BF)
        ties = (returned,) if k == 3 else ()
        right, left = lax.optimization_barrier((right, left, *ties))[:2]
        marks = (right, left)
        right = lax.ppermute(right, "z", RIGHT)
        left = lax.ppermute(left, "z", LEFT)
        right, left = lax.optimization_barrier((right, left))
    right = (chunk(1).astype(F32) + right.astype(F32)).astype(BF)
    left = (chunk(7).astype(F32) + left.astype(F32)).astype(BF)
    return right, left, chunk(0), marks


def reduce_end(right, left, mine, late):
    right, left = lax.optimization_barrier((right, left, late))[:2]
    right = lax.ppermute(right, "z", RIGHT)
    left = lax.ppermute(left, "z", LEFT)
    return mine.astype(F32) + right.astype(F32) + left.astype(F32)


def both_xh(piece):
    return jnp.concatenate([piece, lax.ppermute(piece, "xh", SWAP)], axis=0)


def shift_blocks(value, steps):
    first, last = max(0, -steps), min(512, 512 - steps)
    return lax.ppermute(value, ALL, [(i, i + steps) for i in range(first, last)])


def shards(q, keys, values, label, skip, x, g, picked, mix, retained, weights, out_map):
    core = lax.axis_index("core")
    xh = lax.axis_index("xh")
    w_pad = jnp.pad(weights[0], ((0, SEG - SHARD), (0, DP - F)))
    o_pad = jnp.pad(out_map, ((0, 0), (0, DP - D)))
    w_pair = both_xh(w_pad)
    w_mine = lax.all_gather(w_pair, "z", axis=0, tiled=True)

    plus = (label + 1).astype(jnp.int32)
    marks = jnp.stack([plus // 16, plus % 16], axis=1).astype(BF)
    own = jnp.concatenate(
        [keys, values, jnp.pad(marks, ((0, 0), (0, WIDE - 2 * KV - 2)))], axis=1
    )
    picked_t = order(picked.T, w_pair)
    held = jnp.repeat(retained[:EXPERTS], CAPP)[:, None]
    spot = jnp.arange(DP, dtype=jnp.int32)
    half = spot // HALF
    rest = spot % HALF
    within = rest % SEG
    pair = rest // SEG
    owner = (pair // 2) * 4 + ((pair % 2) ^ xh) * 2 + (half ^ core)
    place = jnp.where(within < SHARD, owner * SHARD + within, -1)[None, :]
    dma = pltpu.SemaphoreType.DMA
    send, sent = call(
        dispatch_kernel,
        "vvvvvv",
        [out((ROWS, SEND)), out((ROWS, TOK))],
        "vh",
        [pltpu.VMEM((ROWS, TOK), BF), dma((1,))],
        2,
    )(picked_t, held, mix.astype(F32).T, place, x.T, g.T)
    got = lax.all_to_all(send.reshape(EXPERTS, CAPP, SEND), CTX, 0, 0, tiled=True)
    own = order(own, send)
    near = shift_blocks(own, 1)
    far = shift_blocks(own, 2)
    shares_shape, qt_shape = (3 * TOK, HEADS * TOK), (HEADS * HD, TOK)
    kt_shape, v_shape = (KV, 3 * TOK), (3 * TOK, KV)
    shares, q_t, k_t, v_win = call(
        shares_kernel,
        "vvvvv",
        [out(shares_shape), out(qt_shape), out(kt_shape), out(v_shape)],
        "hhhh",
        [
            pltpu.VMEM((3 * TOK, WIDE), BF),
            pltpu.VMEM((3 * TOK, 2 * TOK), F32),
            pltpu.VMEM(shares_shape, BF),
            pltpu.VMEM(qt_shape, BF),
            pltpu.VMEM(kt_shape, BF),
            pltpu.VMEM(v_shape, BF),
            dma((7,)),
        ],
        8,
    )(q, far, near, own, plus.astype(F32)[None, :])

    got = order(got, v_win).reshape(ROWS, SEND)
    x_swapped = lax.ppermute(got[:, HALF:DP], "core", SWAP)
    o_pair = both_xh(order(o_pad, v_win))
    o_mine = lax.all_gather(o_pair, "z", axis=0, tiled=True)
    w_mine = order(w_mine, x_swapped, o_pair)
    w_other = lax.ppermute(w_mine, "core", SWAP)
    back, pg = call(
        expert_kernel,
        "vhh",
        [out((ROWS, BACK)), out((ROWS, DP))],
        "hh",
        [
            pltpu.VMEM((HALF, DP), BF),
            pltpu.VMEM((HALF, DP), BF),
            pltpu.VMEM((ROWS, BACK), BF),
            pltpu.VMEM((ROWS, DP), BF),
            pltpu.VMEM((ROWS, DP), F32),
            dma((4,)),
        ],
        3,
    )(got, w_mine, w_other)
    returned = lax.all_to_all(back.reshape(EXPERTS, CAPP, BACK), CTX, 0, 0, tiled=True)
    returned = returned.reshape(ROWS, BACK)

    pg_swapped = lax.ppermute(pg, "core", SWAP)
    partial = call(
        map_kernel,
        "hhhh",
        [out((HALF, DP))],
        "v",
        [
            pltpu.VMEM((ROWS, HALF), BF),
            pltpu.VMEM((ROWS, HALF), BF),
            pltpu.VMEM((ROWS, DP), BF),
            pltpu.VMEM((ROWS, DP), BF),
            dma((4,)),
        ],
        2,
    )(got[:, :HALF], x_swapped, pg, pg_swapped)[0]
    right, left, mine, marks = reduce_start(partial.reshape(8, 2 * SEG, DP), returned)
    o_mine = order(o_mine, *marks)
    o_other = lax.ppermute(o_mine, "core", SWAP)
    src_t, gate_t, sg, far_g, near_g, own_g = call(
        late_kernel,
        "svvvvhhhhhhh",
        [
            out((D, TOK)),
            out((4, TOK), F32),
            out(shares_shape),
            out((TOK, 2 * KV)),
            out((TOK, 2 * KV)),
            out((TOK, 2 * KV), F32),
        ],
        "vvvvvv",
        [
            pltpu.VMEM((DP, TOK), BF),
            pltpu.VMEM((HEADS * HD, TOK), BF),
            pltpu.VMEM((3 * TOK, HD), F32),
            pltpu.VMEM((3 * TOK, HD), F32),
            pltpu.VMEM((ROWS, TOK), BF),
            pltpu.VMEM(v_shape, BF),
            pltpu.VMEM((D, TOK), BF),
            pltpu.VMEM((16 * HD, DP), BF),
            pltpu.VMEM((16 * HD, DP), BF),
            pltpu.VMEM(qt_shape, BF),
            pltpu.VMEM(shares_shape, BF),
            dma((7,)),
        ],
        8,
    )(
        jnp.stack([core, xh]).astype(jnp.int32), picked_t, held, place, returned,
        sent, v_win, skip.T, o_mine, o_other, q_t, shares,
    )
    merged = reduce_end(right, left, mine, near_g)
    away = merged[SEG:].astype(BF)
    map_grad = (merged[:SEG] + lax.ppermute(away, "xh", SWAP).astype(F32)).astype(BF)
    map_grad = map_grad[None, :SHARD, :F]

    got_near = shift_blocks(near_g, -1)
    got_far = shift_blocks(far_g, -2)
    q_grad = call(query_kernel, "vv", [out((TOK, HEADS * HD))], "v", [], 3)(sg, k_t)[0]
    kv_grad = (own_g + got_near.astype(F32) + got_far.astype(F32)).astype(BF)
    return (
        q_grad,
        kv_grad[:, :KV],
        kv_grad[:, KV:],
        src_t.T,
        gate_t.T.astype(BF),
        map_grad,
    )


def solution(mesh):
    fine = Mesh(mesh.devices.reshape(8, 2, 8, 2, 2), ALL)
    rows = P(ALL, None)
    fsdp = ("z", "xh", "core")
    return jax.shard_map(
        shards,
        mesh=fine,
        in_specs=(
            rows, rows, rows, P(ALL), rows, rows, rows, rows, rows, P(),
            P(CTX, fsdp, None), P(fsdp, None),
        ),
        out_specs=(rows, rows, rows, rows, rows, P(CTX, fsdp, None)),
        check_vma=False,
    )
```

```python
import jax
import jax.numpy as jnp
from jax import lax
from jax.experimental import pallas as pl
from jax.experimental.pallas import tpu as pltpu
from jax.sharding import Mesh, PartitionSpec as P

TOK = 128
D = 1440
F = 1440
HEADS = 32
KV_HEADS = 4
HD = 64
CAP = 6
CAPP = 8
EXPERTS = 16
ROWS = EXPERTS * CAPP
SEG = 48
SHARD = 45
DP = 1536
HALF = 768
SEND = 3072
BACK = 1664
KV = 256
WIDE = 640
BF = jnp.bfloat16
F32 = jnp.float32
ALL = ("y", "xl", "z", "xh", "core")
CTX = ("y", "xl")
SWAP = ((0, 1), (1, 0))


def dot(a, b, dims):
    return lax.dot_general(a, b, (dims, ((), ())), preferred_element_type=F32)


SPACES = {"s": pltpu.SMEM, "v": pltpu.VMEM, "h": pltpu.HBM}


def out(shape, dtype=BF):
    return jax.ShapeDtypeStruct(shape, dtype)


def call(kernel, ins, outs, out_spaces, scratch, weight_us):
    return pl.pallas_call(
        kernel,
        out_shape=outs,
        in_specs=[pl.BlockSpec(memory_space=SPACES[k]) for k in ins],
        out_specs=[pl.BlockSpec(memory_space=SPACES[k]) for k in out_spaces],
        scratch_shapes=scratch,
        compiler_params=pltpu.CompilerParams(vmem_limit_bytes=60 * 1024 * 1024),
        cost_estimate=pl.CostEstimate(
            flops=0, bytes_accessed=int(weight_us * 3690000), transcendentals=0
        ),
    )


def copies_of(pairs, sems):
    return [pltpu.make_async_copy(a, b, sems.at[i]) for i, (a, b) in enumerate(pairs)]


def order(value, *ties):
    return lax.optimization_barrier((value, *ties))[0]


def dispatch_kernel(
    picked_ref, held_ref, gate_ref, place_ref, x_ref, g_ref, out_ref, sent_any, sent_ref, sems
):
    held = held_ref[...]
    chosen = [picked_ref[s : s + 1, :] == held for s in range(4)]
    routed = chosen[0] | chosen[1] | chosen[2] | chosen[3]
    routed_f = jnp.where(routed, 1.0, 0.0)
    before = lax.broadcasted_iota(jnp.int32, (TOK, TOK), 0) <= lax.broadcasted_iota(
        jnp.int32, (TOK, TOK), 1
    )
    upper = jnp.where(before, 1.0, 0.0).astype(BF)
    rank = dot(routed_f.astype(BF), upper, ((1,), (0,))) - 1.0
    slot = lax.broadcasted_iota(jnp.int32, (ROWS, TOK), 0) % CAPP
    sent = routed & (rank == slot.astype(F32))
    sent_bf = jnp.where(sent, 1.0, 0.0).astype(BF)
    sent_ref[...] = sent_bf
    copy = pltpu.make_async_copy(sent_ref, sent_any, sems.at[0])
    copy.start()
    gate = jnp.zeros((ROWS, TOK), F32)
    for s in range(4):
        gate = gate + jnp.where(chosen[s] & sent, gate_ref[s : s + 1, :], 0.0)
    gate = jnp.sum(gate, axis=1, keepdims=True)
    rows = dot(sent_bf, x_ref[...], ((1,), (1,))).astype(BF)
    feature = lax.broadcasted_iota(jnp.int32, (D, 256), 0)
    for c in range(DP // 256):
        pick = jnp.where(feature == place_ref[:, c * 256 : (c + 1) * 256], 1.0, 0.0).astype(BF)
        out_ref[:, c * 256 : (c + 1) * 256] = dot(rows, pick, ((1,), (0,))).astype(BF)
    grads = dot(sent_bf, g_ref[...], ((1,), (1,))).astype(BF)
    out_ref[:, DP:] = jnp.concatenate(
        [grads, jnp.broadcast_to(gate, (ROWS, SEND - DP - F)).astype(BF)], axis=1
    )
    copy.wait()


def shares_kernel(
    q_ref, far_ref, near_ref, own_ref, label_ref, shares_any, qt_any, kt_any, v_any,
    kv_s, bias_s, shares_ref, qt_ref, kt_ref, v_ref, sems,
):
    for part, ref in enumerate((far_ref, near_ref, own_ref)):
        kv_s[part * TOK : (part + 1) * TOK, :] = ref[...]
    marks = kv_s[:, 2 * KV :].astype(F32)
    docs = marks[:, 0:1] * 16.0 + marks[:, 1:2]
    r_at = lax.broadcasted_iota(jnp.int32, (3 * TOK, TOK), 0)
    p_at = lax.broadcasted_iota(jnp.int32, (3 * TOK, TOK), 1)
    allowed = (r_at <= 2 * TOK + p_at) & (docs == label_ref[...])
    bias = jnp.where(allowed, 0.0, -1e30)
    bias_s[...] = jnp.concatenate([bias, bias], axis=1)
    v_ref[...] = kv_s[:, KV : 2 * KV]
    for t in range(2):
        kt_ref[t * 128 : (t + 1) * 128, :] = jnp.transpose(
            kv_s[:, t * 128 : (t + 1) * 128].astype(F32)
        ).astype(BF)
    copies = []
    for g in range(KV_HEADS):
        k_one = kv_s[:, g * HD : (g + 1) * HD]

        def pair(i, carry, g=g, k_one=k_one):
            at = pl.multiple_of((g * 4 + i) * 128, 128)
            flipped = jnp.transpose(q_ref[:, pl.ds(at, 128)].astype(F32) * 0.125).astype(BF)
            qt_ref[pl.ds(at, 128), :] = flipped
            q_two = jnp.concatenate([flipped[:HD], flipped[HD:]], axis=1)
            s = dot(k_one, q_two, ((1,), (0,))) + bias_s[...]
            e = jnp.exp(s - jnp.max(s, axis=0, keepdims=True))
            shares = e * (1.0 / jnp.sum(e, axis=0, keepdims=True))
            shares_ref[:, pl.ds(pl.multiple_of(2 * at, 256), 256)] = shares.astype(BF)
            return carry

        lax.fori_loop(0, 4, pair, 0)
        columns = slice(g * 8 * TOK, (g + 1) * 8 * TOK)
        copies.append(
            pltpu.make_async_copy(
                shares_ref.at[:, columns], shares_any.at[:, columns], sems.at[g]
            )
        )
        copies[-1].start()
    pairs = ((qt_ref, qt_any), (kt_ref, kt_any), (v_ref, v_any))
    for i, (source, target) in enumerate(pairs):
        copies.append(pltpu.make_async_copy(source, target, sems.at[4 + i]))
        copies[-1].start()
    for copy in copies:
        copy.wait()


def expert_kernel(
    got_ref, got2_ref, wm_any, wo_any, back_any, part_any,
    wm_ref, wo_ref, back_ref, pg_ref, pre_ref, part_ref, sems,
):
    loads = copies_of(((wm_any, wm_ref), (wo_any, wo_ref)), sems)
    for copy in loads:
        copy.start()
    x_mine = jnp.concatenate([got_ref[:, :HALF], got2_ref[:, HALF:DP]], axis=0)
    x_other = jnp.concatenate([got_ref[:, HALF:DP], got2_ref[:, :HALF]], axis=0)
    for copy in loads:
        copy.wait()
    step = 512
    for lo in range(0, DP, step):
        at = slice(lo, lo + step)
        pre_ref[:, at] = dot(x_mine, wm_ref[:, at], ((1,), (0,))) + dot(
            x_other, wo_ref[:, at], ((1,), (0,))
        )
    gate_at = slice(DP + F, DP + F + 1)
    gate = jnp.concatenate([got_ref[:, gate_at], got2_ref[:, gate_at]], axis=0).astype(F32)
    total = jnp.zeros((2 * ROWS, 1), F32)
    for lo in range(0, DP, step):
        pre = pre_ref[:, lo : lo + step]
        at = slice(DP + lo, DP + lo + step)
        grad = jnp.concatenate([got_ref[:, at], got2_ref[:, at]], axis=0).astype(F32)
        sig = 1.0 / (1.0 + jnp.exp(-pre))
        total = total + jnp.sum(grad * (pre * sig), axis=1, keepdims=True)
        slope = sig * (1.0 + pre * (1.0 - sig))
        pg_ref[:, lo : lo + step] = (gate * grad * slope).astype(BF)
    pg = pg_ref[...]
    stores = []
    for c in range(HALF // 256):
        r = slice(c * 256, (c + 1) * 256)
        part_ref[r, :] = dot(x_mine[:, r], pg, ((0,), (0,))).astype(BF)
        stores.append(
            pltpu.make_async_copy(part_ref.at[r, :], part_any.at[r, :], sems.at[2 + c])
        )
        stores[-1].start()
    pg = pg_ref[:ROWS, :]
    for c in range(HALF // 256):
        r = slice(c * 256, (c + 1) * 256)
        back_ref[:, c * 256 : (c + 1) * 256] = dot(pg, wm_ref[r, :], ((1,), (1,))).astype(BF)
        back_ref[:, HALF + c * 256 : HALF + (c + 1) * 256] = dot(
            pg, wo_ref[r, :], ((1,), (1,))
        ).astype(BF)
    back_ref[:, DP:] = jnp.broadcast_to(total[:ROWS], (ROWS, BACK - DP)).astype(BF)
    stores.append(pltpu.make_async_copy(back_ref, back_any, sems.at[5]))
    stores[-1].start()
    for copy in stores:
        copy.wait()


def late_kernel(
    at_ref, picked_ref, held_ref, place_ref,
    p0, p1, p2, p3, p4, p5, p6, p7, sent_any, v_any, skip_any, om_any, oo_any, qt_any, shares_any,
    src_ref, gate_ref, sg_ref, farg_ref, nearg_ref, owng_ref,
    hidden_s, cot_s, acck_s, accv_s, back_ref,
    sent_ref, v_ref, skip_ref, om_ref, oo_ref, qt_ref, shares_ref, sems,
):
    pairs = (
        (sent_any, sent_ref), (skip_any, skip_ref), (om_any, om_ref), (oo_any, oo_ref),
        (v_any, v_ref), (qt_any, qt_ref), (shares_any, shares_ref),
    )
    copies = copies_of(pairs, sems)
    arrived = []
    for i, piece in enumerate((p0, p1, p2, p3, p4, p5, p6, p7)):
        rows = pl.ds(pl.multiple_of(((at_ref[2] + i) % 8) * 16, 16), 16)
        arrived.append(pltpu.make_async_copy(piece, back_ref.at[rows, :], sems.at[7 + i]))
    for copy in arrived + copies:
        copy.start()
    for copy in arrived:
        copy.wait()
    copies[0].wait()
    sent_bf = sent_ref[...]
    sent = sent_bf.astype(F32) > 0.5
    held = held_ref[...]
    gate_part = back_ref[:, DP : DP + 1].astype(F32)
    for s in range(4):
        mine = (picked_ref[s : s + 1, :] == held) & sent
        gate_ref[s : s + 1, :] = jnp.sum(jnp.where(mine, gate_part, 0.0), axis=0, keepdims=True)
    src = dot(sent_bf, back_ref[:, :DP], ((0,), (0,))).astype(BF)
    feature = lax.broadcasted_iota(jnp.int32, (D, 256), 0)
    total = jnp.zeros((D, TOK), F32)
    for c in range(DP // 256):
        pick = jnp.where(feature == place_ref[:, c * 256 : (c + 1) * 256], 1.0, 0.0).astype(BF)
        total = total + dot(pick, src[:, c * 256 : (c + 1) * 256], ((1,), (1,)))
    src_ref[...] = total.astype(BF)
    copies[1].wait()
    hidden_s[:D, :] = (skip_ref[...].astype(F32) + total).astype(BF)
    hidden_s[D:, :] = jnp.zeros((DP - D, TOK), BF)

    core, xh = at_ref[0], at_ref[1]
    for ref, place, copy in (
        (om_ref, core * HD, copies[2]),
        (oo_ref, HD - core * HD, copies[3]),
    ):
        copy.wait()
        for c in range(4):
            block = dot(ref[c * 256 : (c + 1) * 256, :], hidden_s[...], ((1,), (0,))).astype(BF)
            for j in range(4):
                across = xh if j % 2 == 0 else 1 - xh
                at = pl.multiple_of((c * 2 + j // 2) * 256 + across * 128 + place, HD)
                cot_s[pl.ds(at, HD), :] = block[j * HD : (j + 1) * HD]

    for copy in copies[4:]:
        copy.wait()
    for t in range(2):
        sums = []
        for g in (2 * t, 2 * t + 1):
            v_one = v_ref[:, g * HD : (g + 1) * HD]
            for i in range(4):
                n = g * 4 + i
                rows = slice(n * 128, n * 128 + HD), slice(n * 128 + HD, (n + 1) * 128)
                q_two = jnp.concatenate([qt_ref[rows[0], :], qt_ref[rows[1], :]], axis=1)
                c_two = jnp.concatenate([cot_s[rows[0], :], cot_s[rows[1], :]], axis=1)
                low = shares_ref[:, n * 256 : (n + 1) * 256]
                dp = dot(v_one, c_two, ((1,), (0,)))
                shares = low.astype(F32)
                centre = jnp.sum(shares * dp, axis=0, keepdims=True)
                sg = (shares * (dp - centre)).astype(BF)
                sg_ref[:, n * 256 : (n + 1) * 256] = sg
                ak = dot(sg, q_two, ((1,), (1,)))
                av = dot(low, c_two, ((1,), (1,)))
                if i == 0:
                    acck_s[...] = ak
                    accv_s[...] = av
                else:
                    acck_s[...] += ak
                    accv_s[...] += av
            sums.append((acck_s[...], accv_s[...]))
        for kind in range(2):
            tile = jnp.concatenate([sums[0][kind], sums[1][kind]], axis=1)
            at = slice(kind * KV + t * 128, kind * KV + (t + 1) * 128)
            farg_ref[:, at] = tile[:TOK].astype(BF)
            nearg_ref[:, at] = tile[TOK : 2 * TOK].astype(BF)
            owng_ref[:, at] = tile[2 * TOK :]


def query_kernel(sg_ref, kt_ref, qg_ref):
    for n in range(16):
        g = n // 4
        qg = dot(kt_ref[g * HD : (g + 1) * HD, :], sg_ref[:, n * 256 : (n + 1) * 256], ((1,), (0,)))
        both = jnp.concatenate([qg[:, :TOK], qg[:, TOK:]], axis=0) * 0.125
        qg_ref[:, n * 128 : (n + 1) * 128] = jnp.transpose(both).astype(BF)


def give_back(back):
    y, xl = lax.axis_index("y"), lax.axis_index("xl")
    grid = back.reshape(8, 2, CAPP, BACK)
    turned = jnp.concatenate([grid, grid], axis=0)
    keep = lax.dynamic_slice(turned, (y, xl, 0, 0), (8, 1, CAPP, BACK))
    give = lax.dynamic_slice(turned, (y, 1 - xl, 0, 0), (8, 1, CAPP, BACK))
    got = lax.ppermute(give, "xl", SWAP)
    both = jnp.concatenate(
        [jnp.where(xl == 0, keep, got), jnp.where(xl == 0, got, keep)], axis=1
    ).reshape(8, 2 * CAPP, BACK)
    pieces = [both[0]]
    for k in range(7, 0, -1):
        pieces.append(lax.ppermute(both[k], "y", [(i, (i + k) % 8) for i in range(8)]))
    return pieces


def both_xh(piece, natural):
    other = lax.ppermute(piece, "xh", SWAP)
    if not natural:
        return jnp.concatenate([piece, other], axis=0)
    lower = lax.axis_index("xh") == 0
    return jnp.concatenate(
        [jnp.where(lower, piece, other), jnp.where(lower, other, piece)], axis=0
    )


def shift_blocks(value, steps):
    first, last = max(0, -steps), min(512, 512 - steps)
    return lax.ppermute(value, ALL, [(i, i + steps) for i in range(first, last)])


def shards(q, keys, values, label, skip, x, g, picked, mix, retained, weights, out_map):
    core = lax.axis_index("core")
    xh = lax.axis_index("xh")
    w_pad = jnp.pad(weights[0], ((0, SEG - SHARD), (0, DP - F)))
    o_pad = jnp.pad(out_map, ((0, 0), (0, DP - D)))
    w_pair = both_xh(w_pad, True)
    w_mine = lax.all_gather(w_pair, "z", axis=0, tiled=True)

    plus = (label + 1).astype(jnp.int32)
    marks = jnp.stack([plus // 16, plus % 16], axis=1).astype(BF)
    own = jnp.concatenate(
        [keys, values, jnp.pad(marks, ((0, 0), (0, WIDE - 2 * KV - 2)))], axis=1
    )
    picked_t = order(picked.T, w_pair)
    held = jnp.repeat(retained[:EXPERTS], CAPP)[:, None]
    spot = jnp.arange(DP, dtype=jnp.int32)
    half = spot // HALF
    rest = spot % HALF
    within = rest % SEG
    pair = rest // SEG
    owner = (pair // 2) * 4 + (pair % 2) * 2 + (half ^ core)
    place = jnp.where(within < SHARD, owner * SHARD + within, -1)[None, :]
    dma = pltpu.SemaphoreType.DMA
    send, sent = call(
        dispatch_kernel,
        "vvvvvv",
        [out((ROWS, SEND)), out((ROWS, TOK))],
        "vh",
        [pltpu.VMEM((ROWS, TOK), BF), dma((1,))],
        2,
    )(picked_t, held, mix.astype(F32).T, place, x.T, g.T)
    got = lax.all_to_all(send.reshape(EXPERTS, CAPP, SEND), CTX, 0, 0, tiled=True)
    own = order(own, send)
    near = shift_blocks(own, 1)
    far = shift_blocks(own, 2)
    shares_shape, qt_shape = (3 * TOK, HEADS * TOK), (HEADS * HD, TOK)
    kt_shape, v_shape = (KV, 3 * TOK), (3 * TOK, KV)
    shares, q_t, k_t, v_win = call(
        shares_kernel,
        "vvvvv",
        [out(shares_shape), out(qt_shape), out(kt_shape), out(v_shape)],
        "hhhh",
        [
            pltpu.VMEM((3 * TOK, WIDE), BF),
            pltpu.VMEM((3 * TOK, 2 * TOK), F32),
            pltpu.VMEM(shares_shape, BF),
            pltpu.VMEM(qt_shape, BF),
            pltpu.VMEM(kt_shape, BF),
            pltpu.VMEM(v_shape, BF),
            dma((7,)),
        ],
        8,
    )(q, far, near, own, plus.astype(F32)[None, :])

    got = order(got, v_win).reshape(ROWS, SEND)
    got_other = lax.ppermute(got, "core", SWAP)
    o_pair = both_xh(order(o_pad, send), False)
    o_mine = lax.all_gather(o_pair, "z", axis=0, tiled=True)
    w_mine = order(w_mine, got_other, o_pair)
    w_other = lax.ppermute(w_mine, "core", SWAP)
    back, partial = call(
        expert_kernel,
        "vvhh",
        [out((ROWS, BACK)), out((HALF, DP))],
        "hh",
        [
            pltpu.VMEM((HALF, DP), BF),
            pltpu.VMEM((HALF, DP), BF),
            pltpu.VMEM((ROWS, BACK), BF),
            pltpu.VMEM((2 * ROWS, DP), BF),
            pltpu.VMEM((2 * ROWS, DP), F32),
            pltpu.VMEM((HALF, DP), BF),
            dma((6,)),
        ],
        3,
    )(got, got_other, w_mine, w_other)
    terms = lax.all_to_all(partial.reshape(16, SEG, DP), ("z", "xh"), 0, 0, tiled=True)
    map_grad = jnp.sum(terms.astype(F32), axis=0)[None, :SHARD, :F].astype(BF)

    returned = give_back(back)
    o_mine = order(o_mine, *returned)
    o_other = lax.ppermute(o_mine, "core", SWAP)
    src_t, gate_t, sg, far_g, near_g, own_g = call(
        late_kernel,
        "svvvhhhhhhhhhhhhhhh",
        [
            out((D, TOK)),
            out((4, TOK), F32),
            out(shares_shape),
            out((TOK, 2 * KV)),
            out((TOK, 2 * KV)),
            out((TOK, 2 * KV), F32),
        ],
        "vvvvvv",
        [
            pltpu.VMEM((DP, TOK), BF),
            pltpu.VMEM((HEADS * HD, TOK), BF),
            pltpu.VMEM((3 * TOK, HD), F32),
            pltpu.VMEM((3 * TOK, HD), F32),
            pltpu.VMEM((ROWS, BACK), BF),
            pltpu.VMEM((ROWS, TOK), BF),
            pltpu.VMEM(v_shape, BF),
            pltpu.VMEM((D, TOK), BF),
            pltpu.VMEM((16 * HD, DP), BF),
            pltpu.VMEM((16 * HD, DP), BF),
            pltpu.VMEM(qt_shape, BF),
            pltpu.VMEM(shares_shape, BF),
            dma((15,)),
        ],
        0.1,
    )(
        jnp.stack([core, xh, lax.axis_index("y")]).astype(jnp.int32), picked_t, held, place,
        *returned, sent, v_win, skip.T, o_mine, o_other, q_t, shares,
    )
    got_near = shift_blocks(near_g, -1)
    got_far = shift_blocks(far_g, -2)
    q_grad = call(query_kernel, "vv", [out((TOK, HEADS * HD))], "v", [], 0.1)(sg, k_t)[0]
    kv_grad = (own_g + got_near.astype(F32) + got_far.astype(F32)).astype(BF)
    return (
        q_grad,
        kv_grad[:, :KV],
        kv_grad[:, KV:],
        src_t.T,
        gate_t.T.astype(BF),
        map_grad,
    )


def solution(mesh):
    fine = Mesh(mesh.devices.reshape(8, 2, 8, 2, 2), ALL)
    rows = P(ALL, None)
    fsdp = ("z", "xh", "core")
    return jax.shard_map(
        shards,
        mesh=fine,
        in_specs=(
            rows, rows, rows, P(ALL), rows, rows, rows, rows, rows, P(),
            P(CTX, fsdp, None), P(fsdp, None),
        ),
        out_specs=(rows, rows, rows, rows, rows, P(CTX, fsdp, None)),
        check_vma=False,
    )
```

```python
import jax
import jax.numpy as jnp
from jax import lax
from jax.experimental import pallas as pl
from jax.experimental.pallas import tpu as pltpu
from jax.sharding import Mesh, PartitionSpec as P

TOK = 128
D = 1440
F = 1440
HEADS = 32
KV_HEADS = 4
HD = 64
CAP = 6
CAPP = 8
EXPERTS = 16
ROWS = EXPERTS * CAPP
SEG = 48
SHARD = 45
DP = 1536
HALF = 768
SEND = 3072
BACK = 1664
KV = 256
WIDE = 640
BF = jnp.bfloat16
F32 = jnp.float32
ALL = ("y", "xl", "z", "xh", "core")
CTX = ("y", "xl")
SWAP = ((0, 1), (1, 0))


def dot(a, b, dims):
    return lax.dot_general(a, b, (dims, ((), ())), preferred_element_type=F32)


SPACES = {"s": pltpu.SMEM, "v": pltpu.VMEM, "h": pltpu.HBM}


def out(shape, dtype=BF):
    return jax.ShapeDtypeStruct(shape, dtype)


def call(kernel, ins, outs, out_spaces, scratch, weight_us):
    return pl.pallas_call(
        kernel,
        out_shape=outs,
        in_specs=[pl.BlockSpec(memory_space=SPACES[k]) for k in ins],
        out_specs=[pl.BlockSpec(memory_space=SPACES[k]) for k in out_spaces],
        scratch_shapes=scratch,
        compiler_params=pltpu.CompilerParams(vmem_limit_bytes=60 * 1024 * 1024),
        cost_estimate=pl.CostEstimate(
            flops=0, bytes_accessed=int(weight_us * 3690000), transcendentals=0
        ),
    )


def copies_of(pairs, sems):
    return [pltpu.make_async_copy(a, b, sems.at[i]) for i, (a, b) in enumerate(pairs)]


def order(value, *ties):
    return lax.optimization_barrier((value, *ties))[0]


def dispatch_kernel(
    picked_ref, held_ref, gate_ref, place_ref, x_ref, g_ref, skip_ref, map_ref,
    out_ref, map_out, sent_any, skip_any, sent_ref, skip_s, sems,
):
    held = held_ref[...]
    chosen = [picked_ref[s : s + 1, :] == held for s in range(4)]
    routed = chosen[0] | chosen[1] | chosen[2] | chosen[3]
    routed_f = jnp.where(routed, 1.0, 0.0)
    before = lax.broadcasted_iota(jnp.int32, (TOK, TOK), 0) <= lax.broadcasted_iota(
        jnp.int32, (TOK, TOK), 1
    )
    upper = jnp.where(before, 1.0, 0.0).astype(BF)
    rank = dot(routed_f.astype(BF), upper, ((1,), (0,))) - 1.0
    slot = lax.broadcasted_iota(jnp.int32, (ROWS, TOK), 0) % CAPP
    sent = routed & (rank == slot.astype(F32))
    sent_bf = jnp.where(sent, 1.0, 0.0).astype(BF)
    sent_ref[...] = sent_bf
    copy = pltpu.make_async_copy(sent_ref, sent_any, sems.at[0])
    copy.start()
    gate = jnp.zeros((ROWS, TOK), F32)
    for s in range(4):
        gate = gate + jnp.where(chosen[s] & sent, gate_ref[s : s + 1, :], 0.0)
    gate = jnp.sum(gate, axis=1, keepdims=True)
    rows = dot(sent_bf, x_ref[...], ((1,), (1,))).astype(BF)
    feature = lax.broadcasted_iota(jnp.int32, (D, 256), 0)
    for c in range(DP // 256):
        pick = jnp.where(feature == place_ref[:, c * 256 : (c + 1) * 256], 1.0, 0.0).astype(BF)
        at = slice(c * 256, (c + 1) * 256)
        out_ref[:, at] = dot(rows, pick, ((1,), (0,))).astype(BF)
        map_out[:, at] = dot(map_ref[...], pick, ((1,), (0,))).astype(BF)
        skip_s[:, at] = dot(skip_ref[...], pick, ((0,), (0,))).astype(BF)
    skip_copy = pltpu.make_async_copy(skip_s, skip_any, sems.at[1])
    skip_copy.start()
    grads = dot(sent_bf, g_ref[...], ((1,), (1,))).astype(BF)
    out_ref[:, DP:] = jnp.concatenate(
        [grads, jnp.broadcast_to(gate, (ROWS, SEND - DP - F)).astype(BF)], axis=1
    )
    copy.wait()
    skip_copy.wait()


def shares_kernel(
    q_ref, far_ref, near_ref, own_ref, label_ref, shares_any, qt_any, kt_any, v_any,
    kv_s, bias_s, shares_ref, qt_ref, kt_ref, v_ref, sems,
):
    for part, ref in enumerate((far_ref, near_ref, own_ref)):
        kv_s[part * TOK : (part + 1) * TOK, :] = ref[...]
    marks = kv_s[:, 2 * KV :].astype(F32)
    docs = marks[:, 0:1] * 16.0 + marks[:, 1:2]
    r_at = lax.broadcasted_iota(jnp.int32, (3 * TOK, TOK), 0)
    p_at = lax.broadcasted_iota(jnp.int32, (3 * TOK, TOK), 1)
    allowed = (r_at <= 2 * TOK + p_at) & (docs == label_ref[...])
    bias = jnp.where(allowed, 0.0, -1e30)
    bias_s[...] = jnp.concatenate([bias, bias], axis=1)
    v_ref[...] = kv_s[:, KV : 2 * KV]
    for t in range(2):
        kt_ref[t * 128 : (t + 1) * 128, :] = jnp.transpose(
            kv_s[:, t * 128 : (t + 1) * 128].astype(F32)
        ).astype(BF)
    copies = []
    for g in range(KV_HEADS):
        k_one = kv_s[:, g * HD : (g + 1) * HD]

        def pair(i, carry, g=g, k_one=k_one):
            at = pl.multiple_of((g * 4 + i) * 128, 128)
            flipped = jnp.transpose(q_ref[:, pl.ds(at, 128)].astype(F32) * 0.125).astype(BF)
            qt_ref[pl.ds(at, 128), :] = flipped
            q_two = jnp.concatenate([flipped[:HD], flipped[HD:]], axis=1)
            s = dot(k_one, q_two, ((1,), (0,))) + bias_s[...]
            e = jnp.exp(s - jnp.max(s, axis=0, keepdims=True))
            shares = e * (1.0 / jnp.sum(e, axis=0, keepdims=True))
            shares_ref[:, pl.ds(pl.multiple_of(2 * at, 256), 256)] = shares.astype(BF)
            return carry

        lax.fori_loop(0, 4, pair, 0)
        columns = slice(g * 8 * TOK, (g + 1) * 8 * TOK)
        copies.append(
            pltpu.make_async_copy(
                shares_ref.at[:, columns], shares_any.at[:, columns], sems.at[g]
            )
        )
        copies[-1].start()
    pairs = ((qt_ref, qt_any), (kt_ref, kt_any), (v_ref, v_any))
    for i, (source, target) in enumerate(pairs):
        copies.append(pltpu.make_async_copy(source, target, sems.at[4 + i]))
        copies[-1].start()
    for copy in copies:
        copy.wait()


def expert_kernel(
    got_ref, got2_ref, wo_ref, wm_any, back_any, part_any,
    wm_ref, back_ref, pg_ref, pre_ref, part_ref, sems,
):
    load = pltpu.make_async_copy(wm_any, wm_ref, sems.at[0])
    load.start()
    x_mine = jnp.concatenate([got_ref[:, :HALF], got2_ref[:, HALF:DP]], axis=0)
    x_other = jnp.concatenate([got_ref[:, HALF:DP], got2_ref[:, :HALF]], axis=0)
    load.wait()
    step = 512
    for lo in range(0, DP, step):
        at = slice(lo, lo + step)
        pre_ref[:, at] = dot(x_mine, wm_ref[:, at], ((1,), (0,))) + dot(
            x_other, wo_ref[:, at], ((1,), (0,))
        )
    gate_at = slice(DP + F, DP + F + 1)
    gate = jnp.concatenate([got_ref[:, gate_at], got2_ref[:, gate_at]], axis=0).astype(F32)
    total = jnp.zeros((2 * ROWS, 1), F32)
    for lo in range(0, DP, step):
        pre = pre_ref[:, lo : lo + step]
        at = slice(DP + lo, DP + lo + step)
        grad = jnp.concatenate([got_ref[:, at], got2_ref[:, at]], axis=0).astype(F32)
        sig = 1.0 / (1.0 + jnp.exp(-pre))
        total = total + jnp.sum(grad * (pre * sig), axis=1, keepdims=True)
        slope = sig * (1.0 + pre * (1.0 - sig))
        pg_ref[:, lo : lo + step] = (gate * grad * slope).astype(BF)
    pg = pg_ref[...]
    stores = []
    for c in range(HALF // 256):
        r = slice(c * 256, (c + 1) * 256)
        part_ref[r, :] = dot(x_mine[:, r], pg, ((0,), (0,))).astype(BF)
        stores.append(
            pltpu.make_async_copy(part_ref.at[r, :], part_any.at[r, :], sems.at[2 + c])
        )
        stores[-1].start()
    pg = pg_ref[:ROWS, :]
    for c in range(HALF // 256):
        r = slice(c * 256, (c + 1) * 256)
        back_ref[:, c * 256 : (c + 1) * 256] = dot(pg, wm_ref[r, :], ((1,), (1,))).astype(BF)
        back_ref[:, HALF + c * 256 : HALF + (c + 1) * 256] = dot(
            pg, wo_ref[r, :], ((1,), (1,))
        ).astype(BF)
    back_ref[:, DP:] = jnp.broadcast_to(total[:ROWS], (ROWS, BACK - DP)).astype(BF)
    stores.append(pltpu.make_async_copy(back_ref, back_any, sems.at[5]))
    stores[-1].start()
    for copy in stores:
        copy.wait()


def combine_kernel(
    at_ref, picked_ref, held_ref, back_any, sent_any, skip_any, om_any,
    gate_ref, src_ref, hidden_ref, cot_ref, back_ref, sent_ref, skip_ref, om_ref, sems,
):
    pairs = ((sent_any, sent_ref), (skip_any, skip_ref), (om_any, om_ref))
    copies = copies_of(pairs, sems)
    arrived = []
    for k in range(8):
        rows = pl.ds(pl.multiple_of(((at_ref[2] + 8 - k) % 8) * 16, 16), 16)
        arrived.append(
            pltpu.make_async_copy(
                back_any.at[k * 16 : (k + 1) * 16, :], back_ref.at[rows, :], sems.at[3 + k]
            )
        )
    for copy in arrived + copies:
        copy.start()
    for copy in arrived:
        copy.wait()
    copies[0].wait()
    sent_bf = sent_ref[...]
    sent = sent_bf.astype(F32) > 0.5
    held = held_ref[...]
    gate_part = back_ref[:, DP : DP + 1].astype(F32)
    for s in range(4):
        mine = (picked_ref[s : s + 1, :] == held) & sent
        gate_ref[s : s + 1, :] = jnp.sum(jnp.where(mine, gate_part, 0.0), axis=0, keepdims=True)
    src = dot(sent_bf, back_ref[:, :DP], ((0,), (0,))).astype(BF)
    src_ref[...] = src
    copies[1].wait()
    hidden = (skip_ref[...].astype(F32) + src.astype(F32)).astype(BF)
    hidden_ref[...] = hidden
    copies[2].wait()
    for c in range(4):
        rows = slice(c * 256, (c + 1) * 256)
        cot_ref[rows, :] = dot(om_ref[rows, :], hidden, ((1,), (1,))).astype(BF)


def late_kernel(
    at_ref, cotm_ref, hidden_ref, v_any, oo_any, qt_any, shares_any,
    sg_ref, farg_ref, nearg_ref, owng_ref,
    cot_s, acck_s, accv_s, v_ref, oo_ref, qt_ref, shares_ref, sems,
):
    pairs = ((oo_any, oo_ref), (v_any, v_ref), (qt_any, qt_ref), (shares_any, shares_ref))
    copies = copies_of(pairs, sems)
    for copy in copies:
        copy.start()
    core, xh = at_ref[0], at_ref[1]

    def spread(block, c, place):
        for j in range(4):
            across = xh if j % 2 == 0 else 1 - xh
            at = pl.multiple_of((c * 2 + j // 2) * 256 + across * 128 + place, HD)
            cot_s[pl.ds(at, HD), :] = block[j * HD : (j + 1) * HD]

    for c in range(4):
        spread(cotm_ref[c * 256 : (c + 1) * 256, :], c, core * HD)
    hidden = jnp.concatenate([hidden_ref[:, HALF:], hidden_ref[:, :HALF]], axis=1)
    copies[0].wait()
    for c in range(4):
        rows = slice(c * 256, (c + 1) * 256)
        spread(dot(oo_ref[rows, :], hidden, ((1,), (1,))).astype(BF), c, HD - core * HD)

    for copy in copies[1:]:
        copy.wait()
    for t in range(2):
        sums = []
        for g in (2 * t, 2 * t + 1):
            v_one = v_ref[:, g * HD : (g + 1) * HD]
            for i in range(4):
                n = g * 4 + i
                rows = slice(n * 128, n * 128 + HD), slice(n * 128 + HD, (n + 1) * 128)
                q_two = jnp.concatenate([qt_ref[rows[0], :], qt_ref[rows[1], :]], axis=1)
                c_two = jnp.concatenate([cot_s[rows[0], :], cot_s[rows[1], :]], axis=1)
                low = shares_ref[:, n * 256 : (n + 1) * 256]
                dp = dot(v_one, c_two, ((1,), (0,)))
                shares = low.astype(F32)
                centre = jnp.sum(shares * dp, axis=0, keepdims=True)
                sg = (shares * (dp - centre)).astype(BF)
                sg_ref[:, n * 256 : (n + 1) * 256] = sg
                ak = dot(sg, q_two, ((1,), (1,)))
                av = dot(low, c_two, ((1,), (1,)))
                if i == 0:
                    acck_s[...] = ak
                    accv_s[...] = av
                else:
                    acck_s[...] += ak
                    accv_s[...] += av
            sums.append((acck_s[...], accv_s[...]))
        for kind in range(2):
            tile = jnp.concatenate([sums[0][kind], sums[1][kind]], axis=1)
            at = slice(kind * KV + t * 128, kind * KV + (t + 1) * 128)
            farg_ref[:, at] = tile[:TOK].astype(BF)
            nearg_ref[:, at] = tile[TOK : 2 * TOK].astype(BF)
            owng_ref[:, at] = tile[2 * TOK :]


def query_kernel(sg_ref, kt_ref, src_ref, place_ref, qg_ref, out_ref):
    for n in range(16):
        g = n // 4
        qg = dot(kt_ref[g * HD : (g + 1) * HD, :], sg_ref[:, n * 256 : (n + 1) * 256], ((1,), (0,)))
        both = jnp.concatenate([qg[:, :TOK], qg[:, TOK:]], axis=0) * 0.125
        qg_ref[:, n * 128 : (n + 1) * 128] = jnp.transpose(both).astype(BF)
    feature = lax.broadcasted_iota(jnp.int32, (D, 256), 0)
    total = jnp.zeros((D, TOK), F32)
    for c in range(DP // 256):
        at = slice(c * 256, (c + 1) * 256)
        pick = jnp.where(feature == place_ref[:, at], 1.0, 0.0).astype(BF)
        total = total + dot(pick, src_ref[:, at], ((1,), (1,)))
    out_ref[...] = total.astype(BF)


def give_back(back):
    y, xl = lax.axis_index("y"), lax.axis_index("xl")
    grid = back.reshape(8, 2, CAPP, BACK)
    turned = jnp.concatenate([grid, grid], axis=0)
    keep = lax.dynamic_slice(turned, (y, xl, 0, 0), (8, 1, CAPP, BACK))
    give = lax.dynamic_slice(turned, (y, 1 - xl, 0, 0), (8, 1, CAPP, BACK))
    got = lax.ppermute(give, "xl", SWAP)
    both = jnp.concatenate(
        [jnp.where(xl == 0, keep, got), jnp.where(xl == 0, got, keep)], axis=1
    )
    both = both.reshape(2, 2, 2, 2 * CAPP, BACK)
    for bit, axis in ((1, 2), (2, 1), (4, 0)):
        stay = lax.slice_in_dim(both, 0, 1, axis=axis)
        move = lax.slice_in_dim(both, 1, 2, axis=axis)
        move = lax.ppermute(move, "y", [(i, (i + bit) % 8) for i in range(8)])
        both = jnp.concatenate([stay, move], axis=axis)
    return both.reshape(ROWS, BACK)


def both_xh(piece):
    other = lax.ppermute(piece, "xh", SWAP)
    lower = lax.axis_index("xh") == 0
    return jnp.concatenate(
        [jnp.where(lower, piece, other), jnp.where(lower, other, piece)], axis=0
    )


def shift_blocks(value, steps):
    first, last = max(0, -steps), min(512, 512 - steps)
    return lax.ppermute(value, ALL, [(i, i + steps) for i in range(first, last)])


def shards(q, keys, values, label, skip, x, g, picked, mix, retained, weights, out_map):
    core = lax.axis_index("core")
    xh = lax.axis_index("xh")
    w_pad = jnp.pad(weights[0], ((0, SEG - SHARD), (0, DP - F)))
    w_pair = both_xh(w_pad)
    w_mine = lax.all_gather(w_pair, "z", axis=0, tiled=True)

    plus = (label + 1).astype(jnp.int32)
    marks = jnp.stack([plus // 16, plus % 16], axis=1).astype(BF)
    own = jnp.concatenate(
        [keys, values, jnp.pad(marks, ((0, 0), (0, WIDE - 2 * KV - 2)))], axis=1
    )
    picked_t = order(picked.T, w_pair)
    held = jnp.repeat(retained[:EXPERTS], CAPP)[:, None]
    column = jnp.arange(DP, dtype=jnp.int32)
    half = column // HALF
    rest = column % HALF
    within = rest % SEG
    pair = rest // SEG
    owner = (pair // 2) * 4 + (pair % 2) * 2 + (half ^ core)
    place = jnp.where(within < SHARD, owner * SHARD + within, -1)[None, :]
    dma = pltpu.SemaphoreType.DMA
    send, o_placed, sent, skip_placed = call(
        dispatch_kernel,
        "vvvvvvvv",
        [out((ROWS, SEND)), out((HD, DP)), out((ROWS, TOK)), out((TOK, DP))],
        "vvhh",
        [pltpu.VMEM((ROWS, TOK), BF), pltpu.VMEM((TOK, DP), BF), dma((2,))],
        2,
    )(picked_t, held, mix.astype(F32).T, place, x.T, g.T, skip.T, out_map)
    got = lax.all_to_all(send.reshape(EXPERTS, CAPP, SEND), CTX, 0, 0, tiled=True)
    own = order(own, send)
    near = shift_blocks(own, 1)
    far = shift_blocks(own, 2)
    o_across = lax.ppermute(o_placed, "xh", SWAP)
    near, far, o_across = lax.optimization_barrier((near, far, o_across))
    shares_shape, qt_shape = (3 * TOK, HEADS * TOK), (HEADS * HD, TOK)
    kt_shape, v_shape = (KV, 3 * TOK), (3 * TOK, KV)
    shares, q_t, k_t, v_win = call(
        shares_kernel,
        "vvvvv",
        [out(shares_shape), out(qt_shape), out(kt_shape), out(v_shape)],
        "hhhh",
        [
            pltpu.VMEM((3 * TOK, WIDE), BF),
            pltpu.VMEM((3 * TOK, 2 * TOK), F32),
            pltpu.VMEM(shares_shape, BF),
            pltpu.VMEM(qt_shape, BF),
            pltpu.VMEM(kt_shape, BF),
            pltpu.VMEM(v_shape, BF),
            dma((7,)),
        ],
        8,
    )(q, far, near, own, plus.astype(F32)[None, :])

    got = order(got, v_win).reshape(ROWS, SEND)
    got_other = lax.ppermute(got, "core", SWAP)
    o_pair = jnp.concatenate([o_placed, o_across], axis=0)
    o_mine = lax.all_gather(o_pair, "z", axis=0, tiled=True)
    w_mine = order(w_mine, got_other, o_pair)
    w_other = lax.ppermute(w_mine, "core", SWAP)
    back, partial = call(
        expert_kernel,
        "vvvh",
        [out((ROWS, BACK)), out((HALF, DP))],
        "hh",
        [
            pltpu.VMEM((HALF, DP), BF),
            pltpu.VMEM((ROWS, BACK), BF),
            pltpu.VMEM((2 * ROWS, DP), BF),
            pltpu.VMEM((2 * ROWS, DP), F32),
            pltpu.VMEM((HALF, DP), BF),
            dma((6,)),
        ],
        3,
    )(got, got_other, w_other, w_mine)
    terms = lax.all_to_all(partial.reshape(16, SEG, DP), ("z", "xh"), 0, 0, tiled=True)
    map_grad = jnp.sum(terms.astype(F32), axis=0)[None, :SHARD, :F].astype(BF)

    returned = give_back(back)
    o_mine = order(o_mine, returned)
    o_other = lax.ppermute(o_mine, "core", SWAP)
    spot = jnp.stack([core, xh, lax.axis_index("y")]).astype(jnp.int32)
    half_shape = (16 * HD, DP)
    gate_t, src, hidden, cot_mine = call(
        combine_kernel,
        "svvhhhh",
        [out((4, TOK), F32), out((TOK, DP)), out((TOK, DP)), out((16 * HD, TOK))],
        "vvvv",
        [
            pltpu.VMEM((ROWS, BACK), BF),
            pltpu.VMEM((ROWS, TOK), BF),
            pltpu.VMEM((TOK, DP), BF),
            pltpu.VMEM(half_shape, BF),
            dma((11,)),
        ],
        3,
    )(spot, picked_t, held, returned, sent, skip_placed, o_mine)
    sg, far_g, near_g, own_g = call(
        late_kernel,
        "svvhhhh",
        [
            out(shares_shape),
            out((TOK, 2 * KV)),
            out((TOK, 2 * KV)),
            out((TOK, 2 * KV), F32),
        ],
        "vvvv",
        [
            pltpu.VMEM((HEADS * HD, TOK), BF),
            pltpu.VMEM((3 * TOK, HD), F32),
            pltpu.VMEM((3 * TOK, HD), F32),
            pltpu.VMEM(v_shape, BF),
            pltpu.VMEM(half_shape, BF),
            pltpu.VMEM(qt_shape, BF),
            pltpu.VMEM(shares_shape, BF),
            dma((4,)),
        ],
        0.1,
    )(spot, cot_mine, hidden, v_win, o_other, q_t, shares)
    got_near = shift_blocks(near_g, -1)
    got_far = shift_blocks(far_g, -2)
    q_grad, src_t = call(
        query_kernel, "vvvv", [out((TOK, HEADS * HD)), out((D, TOK))], "vv", [], 0.1
    )(sg, k_t, src, place)
    kv_grad = (own_g + got_near.astype(F32) + got_far.astype(F32)).astype(BF)
    return (
        q_grad,
        kv_grad[:, :KV],
        kv_grad[:, KV:],
        src_t.T,
        gate_t.T.astype(BF),
        map_grad,
    )


def solution(mesh):
    fine = Mesh(mesh.devices.reshape(8, 2, 8, 2, 2), ALL)
    rows = P(ALL, None)
    fsdp = ("z", "xh", "core")
    return jax.shard_map(
        shards,
        mesh=fine,
        in_specs=(
            rows, rows, rows, P(ALL), rows, rows, rows, rows, rows, P(),
            P(CTX, fsdp, None), P(fsdp, None),
        ),
        out_specs=(rows, rows, rows, rows, rows, P(CTX, fsdp, None)),
        check_vma=False,
    )
```

```python
import jax
import jax.numpy as jnp
from jax import lax
from jax.experimental import pallas as pl
from jax.experimental.pallas import tpu as pltpu
from jax.sharding import Mesh, PartitionSpec as P

TOK = 128
D = 1440
F = 1440
HEADS = 32
KV_HEADS = 4
HD = 64
CAP = 6
CAPP = 8
EXPERTS = 16
ROWS = EXPERTS * CAPP
SEG = 48
SHARD = 45
DP = 1536
HALF = 768
SEND = 3072
BACK = 1664
KV = 256
WIDE = 640
BF = jnp.bfloat16
F32 = jnp.float32
ALL = ("y", "xl", "z", "xh", "core")
CTX = ("y", "xl")
SWAP = ((0, 1), (1, 0))


def dot(a, b, dims):
    return lax.dot_general(a, b, (dims, ((), ())), preferred_element_type=F32)


SPACES = {"s": pltpu.SMEM, "v": pltpu.VMEM, "h": pltpu.HBM}


def out(shape, dtype=BF):
    return jax.ShapeDtypeStruct(shape, dtype)


def call(kernel, ins, outs, out_spaces, scratch, weight_us):
    return pl.pallas_call(
        kernel,
        out_shape=outs,
        in_specs=[pl.BlockSpec(memory_space=SPACES[k]) for k in ins],
        out_specs=[pl.BlockSpec(memory_space=SPACES[k]) for k in out_spaces],
        scratch_shapes=scratch,
        compiler_params=pltpu.CompilerParams(vmem_limit_bytes=60 * 1024 * 1024),
        cost_estimate=pl.CostEstimate(
            flops=0, bytes_accessed=int(weight_us * 3690000), transcendentals=0
        ),
    )


def copies_of(pairs, sems):
    return [pltpu.make_async_copy(a, b, sems.at[i]) for i, (a, b) in enumerate(pairs)]


def order(value, *ties):
    return lax.optimization_barrier((value, *ties))[0]


def dispatch_kernel(
    picked_ref, held_ref, gate_ref, place_ref, x_ref, g_ref, skip_ref, map_ref,
    out_ref, map_out, sent_any, skip_any, sent_ref, skip_s, sems,
):
    held = held_ref[...]
    chosen = [picked_ref[s : s + 1, :] == held for s in range(4)]
    routed = chosen[0] | chosen[1] | chosen[2] | chosen[3]
    routed_f = jnp.where(routed, 1.0, 0.0)
    before = lax.broadcasted_iota(jnp.int32, (TOK, TOK), 0) <= lax.broadcasted_iota(
        jnp.int32, (TOK, TOK), 1
    )
    upper = jnp.where(before, 1.0, 0.0).astype(BF)
    rank = dot(routed_f.astype(BF), upper, ((1,), (0,))) - 1.0
    slot = lax.broadcasted_iota(jnp.int32, (ROWS, TOK), 0) % CAPP
    sent = routed & (rank == slot.astype(F32))
    sent_bf = jnp.where(sent, 1.0, 0.0).astype(BF)
    sent_ref[...] = sent_bf
    copy = pltpu.make_async_copy(sent_ref, sent_any, sems.at[0])
    copy.start()
    gate = jnp.zeros((ROWS, TOK), F32)
    for s in range(4):
        gate = gate + jnp.where(chosen[s] & sent, gate_ref[s : s + 1, :], 0.0)
    gate = jnp.sum(gate, axis=1, keepdims=True)
    rows = dot(sent_bf, x_ref[...], ((1,), (1,))).astype(BF)
    feature = lax.broadcasted_iota(jnp.int32, (D, 256), 0)
    for c in range(DP // 256):
        pick = jnp.where(feature == place_ref[:, c * 256 : (c + 1) * 256], 1.0, 0.0).astype(BF)
        at = slice(c * 256, (c + 1) * 256)
        out_ref[:, at] = dot(rows, pick, ((1,), (0,))).astype(BF)
        map_out[:, at] = dot(map_ref[...], pick, ((1,), (0,))).astype(BF)
        skip_s[:, at] = dot(skip_ref[...], pick, ((0,), (0,))).astype(BF)
    skip_copy = pltpu.make_async_copy(skip_s, skip_any, sems.at[1])
    skip_copy.start()
    grads = dot(sent_bf, g_ref[...], ((1,), (1,))).astype(BF)
    out_ref[:, DP:] = jnp.concatenate(
        [grads, jnp.broadcast_to(gate, (ROWS, SEND - DP - F)).astype(BF)], axis=1
    )
    copy.wait()
    skip_copy.wait()


def shares_kernel(
    q_ref, far_ref, near_ref, own_ref, label_ref, shares_any, qt_any, kt_any, v_any,
    kv_s, bias_s, shares_ref, qt_ref, kt_ref, v_ref, sems,
):
    for part, ref in enumerate((far_ref, near_ref, own_ref)):
        kv_s[part * TOK : (part + 1) * TOK, :] = ref[...]
    marks = kv_s[:, 2 * KV :].astype(F32)
    docs = marks[:, 0:1] * 16.0 + marks[:, 1:2]
    r_at = lax.broadcasted_iota(jnp.int32, (3 * TOK, TOK), 0)
    p_at = lax.broadcasted_iota(jnp.int32, (3 * TOK, TOK), 1)
    allowed = (r_at <= 2 * TOK + p_at) & (docs == label_ref[...])
    bias = jnp.where(allowed, 0.0, -1e30)
    bias_s[...] = jnp.concatenate([bias, bias], axis=1)
    v_ref[...] = kv_s[:, KV : 2 * KV]
    for t in range(2):
        kt_ref[t * 128 : (t + 1) * 128, :] = jnp.transpose(
            kv_s[:, t * 128 : (t + 1) * 128].astype(F32)
        ).astype(BF)
    copies = []
    for g in range(KV_HEADS):
        k_one = kv_s[:, g * HD : (g + 1) * HD]

        def pair(i, carry, g=g, k_one=k_one):
            at = pl.multiple_of((g * 4 + i) * 128, 128)
            flipped = jnp.transpose(q_ref[:, pl.ds(at, 128)].astype(F32) * 0.125).astype(BF)
            qt_ref[pl.ds(at, 128), :] = flipped
            q_two = jnp.concatenate([flipped[:HD], flipped[HD:]], axis=1)
            s = dot(k_one, q_two, ((1,), (0,))) + bias_s[...]
            e = jnp.exp(s - jnp.max(s, axis=0, keepdims=True))
            shares = e * (1.0 / jnp.sum(e, axis=0, keepdims=True))
            shares_ref[:, pl.ds(pl.multiple_of(2 * at, 256), 256)] = shares.astype(BF)
            return carry

        lax.fori_loop(0, 4, pair, 0)
        columns = slice(g * 8 * TOK, (g + 1) * 8 * TOK)
        copies.append(
            pltpu.make_async_copy(
                shares_ref.at[:, columns], shares_any.at[:, columns], sems.at[g]
            )
        )
        copies[-1].start()
    pairs = ((qt_ref, qt_any), (kt_ref, kt_any), (v_ref, v_any))
    for i, (source, target) in enumerate(pairs):
        copies.append(pltpu.make_async_copy(source, target, sems.at[4 + i]))
        copies[-1].start()
    for copy in copies:
        copy.wait()


def expert_kernel(
    got_ref, got2_ref, wo_ref, wm_any, back_any, pg_any, x_any,
    wm_ref, back_ref, pg_ref, x_ref, pre_ref, sems,
):
    load = pltpu.make_async_copy(wm_any, wm_ref, sems.at[0])
    load.start()
    x_mine = jnp.concatenate([got_ref[:, :HALF], got2_ref[:, HALF:DP]], axis=0)
    x_other = jnp.concatenate([got_ref[:, HALF:DP], got2_ref[:, :HALF]], axis=0)
    x_ref[...] = x_mine
    stores = [pltpu.make_async_copy(x_ref, x_any, sems.at[1])]
    stores[0].start()
    load.wait()
    step = 512
    for lo in range(0, DP, step):
        at = slice(lo, lo + step)
        pre_ref[:, at] = dot(x_mine, wm_ref[:, at], ((1,), (0,))) + dot(
            x_other, wo_ref[:, at], ((1,), (0,))
        )
    gate_at = slice(DP + F, DP + F + 1)
    gate = jnp.concatenate([got_ref[:, gate_at], got2_ref[:, gate_at]], axis=0).astype(F32)
    total = jnp.zeros((2 * ROWS, 1), F32)
    for lo in range(0, DP, step):
        pre = pre_ref[:, lo : lo + step]
        at = slice(DP + lo, DP + lo + step)
        grad = jnp.concatenate([got_ref[:, at], got2_ref[:, at]], axis=0).astype(F32)
        sig = 1.0 / (1.0 + jnp.exp(-pre))
        total = total + jnp.sum(grad * (pre * sig), axis=1, keepdims=True)
        slope = sig * (1.0 + pre * (1.0 - sig))
        pg_ref[:, lo : lo + step] = (gate * grad * slope).astype(BF)
    stores.append(pltpu.make_async_copy(pg_ref, pg_any, sems.at[2]))
    stores[1].start()
    pg = pg_ref[:ROWS, :]
    for c in range(HALF // 256):
        r = slice(c * 256, (c + 1) * 256)
        back_ref[:, c * 256 : (c + 1) * 256] = dot(pg, wm_ref[r, :], ((1,), (1,))).astype(BF)
        back_ref[:, HALF + c * 256 : HALF + (c + 1) * 256] = dot(
            pg, wo_ref[r, :], ((1,), (1,))
        ).astype(BF)
    back_ref[:, DP:] = jnp.broadcast_to(total[:ROWS], (ROWS, BACK - DP)).astype(BF)
    stores.append(pltpu.make_async_copy(back_ref, back_any, sems.at[3]))
    stores[2].start()
    for copy in stores:
        copy.wait()


def map_kernel(x_any, pg_any, part_any, x_ref, pg_ref, part_ref, sems):
    loads = copies_of(((x_any, x_ref), (pg_any, pg_ref)), sems)
    for copy in loads:
        copy.start()
    for copy in loads:
        copy.wait()
    stores = []
    for c in range(HALF // 256):
        r = slice(c * 256, (c + 1) * 256)
        part_ref[r, :] = dot(x_ref[:, r], pg_ref[...], ((0,), (0,))).astype(BF)
        stores.append(
            pltpu.make_async_copy(part_ref.at[r, :], part_any.at[r, :], sems.at[2 + c])
        )
        stores[-1].start()
    for copy in stores:
        copy.wait()


def combine_kernel(
    picked_ref, held_ref, back_any, sent_any, skip_any, om_any,
    gate_ref, src_ref, hidden_ref, cot_ref, back_ref, sent_ref, skip_ref, om_ref, sems,
):
    pairs = (
        (sent_any, sent_ref), (skip_any, skip_ref), (om_any, om_ref), (back_any, back_ref)
    )
    copies = copies_of(pairs, sems)
    for copy in copies:
        copy.start()
    copies[3].wait()
    copies[0].wait()
    sent_bf = sent_ref[...]
    sent = sent_bf.astype(F32) > 0.5
    held = held_ref[...]
    gate_part = back_ref[:, DP : DP + 1].astype(F32)
    for s in range(4):
        mine = (picked_ref[s : s + 1, :] == held) & sent
        gate_ref[s : s + 1, :] = jnp.sum(jnp.where(mine, gate_part, 0.0), axis=0, keepdims=True)
    src = dot(sent_bf, back_ref[:, :DP], ((0,), (0,))).astype(BF)
    src_ref[...] = src
    copies[1].wait()
    hidden = (skip_ref[...].astype(F32) + src.astype(F32)).astype(BF)
    hidden_ref[...] = hidden
    copies[2].wait()
    for c in range(4):
        rows = slice(c * 256, (c + 1) * 256)
        cot_ref[rows, :] = dot(om_ref[rows, :], hidden, ((1,), (1,))).astype(BF)


def late_kernel(
    at_ref, cotm_ref, hidden_ref, v_any, oo_any, qt_any, shares_any,
    sg_ref, farg_ref, nearg_ref, owng_ref,
    cot_s, acck_s, accv_s, v_ref, oo_ref, qt_ref, shares_ref, sems,
):
    pairs = ((oo_any, oo_ref), (v_any, v_ref), (qt_any, qt_ref), (shares_any, shares_ref))
    copies = copies_of(pairs, sems)
    for copy in copies:
        copy.start()
    core, xh = at_ref[0], at_ref[1]

    def spread(block, c, place):
        for j in range(4):
            across = xh if j % 2 == 0 else 1 - xh
            at = pl.multiple_of((c * 2 + j // 2) * 256 + across * 128 + place, HD)
            cot_s[pl.ds(at, HD), :] = block[j * HD : (j + 1) * HD]

    for c in range(4):
        spread(cotm_ref[c * 256 : (c + 1) * 256, :], c, core * HD)
    hidden = jnp.concatenate([hidden_ref[:, HALF:], hidden_ref[:, :HALF]], axis=1)
    copies[0].wait()
    for c in range(4):
        rows = slice(c * 256, (c + 1) * 256)
        spread(dot(oo_ref[rows, :], hidden, ((1,), (1,))).astype(BF), c, HD - core * HD)

    for copy in copies[1:]:
        copy.wait()
    for t in range(2):
        sums = []
        for g in (2 * t, 2 * t + 1):
            v_one = v_ref[:, g * HD : (g + 1) * HD]
            for i in range(4):
                n = g * 4 + i
                rows = slice(n * 128, n * 128 + HD), slice(n * 128 + HD, (n + 1) * 128)
                q_two = jnp.concatenate([qt_ref[rows[0], :], qt_ref[rows[1], :]], axis=1)
                c_two = jnp.concatenate([cot_s[rows[0], :], cot_s[rows[1], :]], axis=1)
                low = shares_ref[:, n * 256 : (n + 1) * 256]
                dp = dot(v_one, c_two, ((1,), (0,)))
                shares = low.astype(F32)
                centre = jnp.sum(shares * dp, axis=0, keepdims=True)
                sg = (shares * (dp - centre)).astype(BF)
                sg_ref[:, n * 256 : (n + 1) * 256] = sg
                ak = dot(sg, q_two, ((1,), (1,)))
                av = dot(low, c_two, ((1,), (1,)))
                if i == 0:
                    acck_s[...] = ak
                    accv_s[...] = av
                else:
                    acck_s[...] += ak
                    accv_s[...] += av
            sums.append((acck_s[...], accv_s[...]))
        for kind in range(2):
            tile = jnp.concatenate([sums[0][kind], sums[1][kind]], axis=1)
            at = slice(kind * KV + t * 128, kind * KV + (t + 1) * 128)
            farg_ref[:, at] = tile[:TOK].astype(BF)
            nearg_ref[:, at] = tile[TOK : 2 * TOK].astype(BF)
            owng_ref[:, at] = tile[2 * TOK :]


def query_kernel(sg_ref, kt_ref, src_ref, place_ref, qg_ref, out_ref):
    for n in range(16):
        g = n // 4
        qg = dot(kt_ref[g * HD : (g + 1) * HD, :], sg_ref[:, n * 256 : (n + 1) * 256], ((1,), (0,)))
        both = jnp.concatenate([qg[:, :TOK], qg[:, TOK:]], axis=0) * 0.125
        qg_ref[:, n * 128 : (n + 1) * 128] = jnp.transpose(both).astype(BF)
    feature = lax.broadcasted_iota(jnp.int32, (D, 256), 0)
    total = jnp.zeros((D, TOK), F32)
    for c in range(DP // 256):
        at = slice(c * 256, (c + 1) * 256)
        pick = jnp.where(feature == place_ref[:, at], 1.0, 0.0).astype(BF)
        total = total + dot(pick, src_ref[:, at], ((1,), (1,)))
    out_ref[...] = total.astype(BF)


def both_xh(piece):
    other = lax.ppermute(piece, "xh", SWAP)
    lower = lax.axis_index("xh") == 0
    return jnp.concatenate(
        [jnp.where(lower, piece, other), jnp.where(lower, other, piece)], axis=0
    )


def shift_blocks(value, steps):
    first, last = max(0, -steps), min(512, 512 - steps)
    return lax.ppermute(value, ALL, [(i, i + steps) for i in range(first, last)])


def shards(q, keys, values, label, skip, x, g, picked, mix, retained, weights, out_map):
    core = lax.axis_index("core")
    xh = lax.axis_index("xh")
    w_pad = jnp.pad(weights[0], ((0, SEG - SHARD), (0, DP - F)))
    w_pair = both_xh(w_pad)
    w_mine = lax.all_gather(w_pair, "z", axis=0, tiled=True)

    plus = (label + 1).astype(jnp.int32)
    marks = jnp.stack([plus // 16, plus % 16], axis=1).astype(BF)
    own = jnp.concatenate(
        [keys, values, jnp.pad(marks, ((0, 0), (0, WIDE - 2 * KV - 2)))], axis=1
    )
    picked_t = order(picked.T, w_pair)
    held = jnp.repeat(retained[:EXPERTS], CAPP)[:, None]
    column = jnp.arange(DP, dtype=jnp.int32)
    half = column // HALF
    rest = column % HALF
    within = rest % SEG
    pair = rest // SEG
    owner = (pair // 2) * 4 + (pair % 2) * 2 + (half ^ core)
    place = jnp.where(within < SHARD, owner * SHARD + within, -1)[None, :]
    dma = pltpu.SemaphoreType.DMA
    send, o_placed, sent, skip_placed = call(
        dispatch_kernel,
        "vvvvvvvv",
        [out((ROWS, SEND)), out((HD, DP)), out((ROWS, TOK)), out((TOK, DP))],
        "vvhh",
        [pltpu.VMEM((ROWS, TOK), BF), pltpu.VMEM((TOK, DP), BF), dma((2,))],
        2,
    )(picked_t, held, mix.astype(F32).T, place, x.T, g.T, skip.T, out_map)
    got = lax.all_to_all(send.reshape(EXPERTS, CAPP, SEND), CTX, 0, 0, tiled=True)
    own = order(own, send)
    near = shift_blocks(own, 1)
    far = shift_blocks(own, 2)
    o_across = lax.ppermute(o_placed, "xh", SWAP)
    near, far, o_across = lax.optimization_barrier((near, far, o_across))
    shares_shape, qt_shape = (3 * TOK, HEADS * TOK), (HEADS * HD, TOK)
    kt_shape, v_shape = (KV, 3 * TOK), (3 * TOK, KV)
    shares, q_t, k_t, v_win = call(
        shares_kernel,
        "vvvvv",
        [out(shares_shape), out(qt_shape), out(kt_shape), out(v_shape)],
        "hhhh",
        [
            pltpu.VMEM((3 * TOK, WIDE), BF),
            pltpu.VMEM((3 * TOK, 2 * TOK), F32),
            pltpu.VMEM(shares_shape, BF),
            pltpu.VMEM(qt_shape, BF),
            pltpu.VMEM(kt_shape, BF),
            pltpu.VMEM(v_shape, BF),
            dma((7,)),
        ],
        8,
    )(q, far, near, own, plus.astype(F32)[None, :])

    got = order(got, v_win).reshape(ROWS, SEND)
    got_other = lax.ppermute(got, "core", SWAP)
    o_pair = jnp.concatenate([o_placed, o_across], axis=0)
    o_mine = lax.all_gather(o_pair, "z", axis=0, tiled=True)
    w_mine = order(w_mine, got_other, o_pair)
    w_other = lax.ppermute(w_mine, "core", SWAP)
    back, pg, x_mine = call(
        expert_kernel,
        "vvvh",
        [out((ROWS, BACK)), out((2 * ROWS, DP)), out((2 * ROWS, HALF))],
        "hhh",
        [
            pltpu.VMEM((HALF, DP), BF),
            pltpu.VMEM((ROWS, BACK), BF),
            pltpu.VMEM((2 * ROWS, DP), BF),
            pltpu.VMEM((2 * ROWS, HALF), BF),
            pltpu.VMEM((2 * ROWS, DP), F32),
            dma((4,)),
        ],
        3,
    )(got, got_other, w_other, w_mine)
    returned = lax.all_to_all(back.reshape(EXPERTS, CAPP, BACK), CTX, 0, 0, tiled=True)
    returned = returned.reshape(ROWS, BACK)
    partial = call(
        map_kernel,
        "hh",
        [out((HALF, DP))],
        "h",
        [
            pltpu.VMEM((2 * ROWS, HALF), BF),
            pltpu.VMEM((2 * ROWS, DP), BF),
            pltpu.VMEM((HALF, DP), BF),
            dma((5,)),
        ],
        3,
    )(x_mine, pg)[0]
    partial = order(partial, returned)
    terms = lax.all_to_all(partial.reshape(16, SEG, DP), ("z", "xh"), 0, 0, tiled=True)
    map_grad = jnp.sum(terms.astype(F32), axis=0)[None, :SHARD, :F].astype(BF)

    o_mine = order(o_mine, returned)
    o_other = lax.ppermute(o_mine, "core", SWAP)
    spot = jnp.stack([core, xh]).astype(jnp.int32)
    half_shape = (16 * HD, DP)
    gate_t, src, hidden, cot_mine = call(
        combine_kernel,
        "vvhhhh",
        [out((4, TOK), F32), out((TOK, DP)), out((TOK, DP)), out((16 * HD, TOK))],
        "vvvv",
        [
            pltpu.VMEM((ROWS, BACK), BF),
            pltpu.VMEM((ROWS, TOK), BF),
            pltpu.VMEM((TOK, DP), BF),
            pltpu.VMEM(half_shape, BF),
            dma((4,)),
        ],
        3,
    )(picked_t, held, returned, sent, skip_placed, o_mine)
    sg, far_g, near_g, own_g = call(
        late_kernel,
        "svvhhhh",
        [
            out(shares_shape),
            out((TOK, 2 * KV)),
            out((TOK, 2 * KV)),
            out((TOK, 2 * KV), F32),
        ],
        "vvvv",
        [
            pltpu.VMEM((HEADS * HD, TOK), BF),
            pltpu.VMEM((3 * TOK, HD), F32),
            pltpu.VMEM((3 * TOK, HD), F32),
            pltpu.VMEM(v_shape, BF),
            pltpu.VMEM(half_shape, BF),
            pltpu.VMEM(qt_shape, BF),
            pltpu.VMEM(shares_shape, BF),
            dma((4,)),
        ],
        0.1,
    )(spot, cot_mine, hidden, v_win, o_other, q_t, shares)
    got_near = shift_blocks(near_g, -1)
    got_far = shift_blocks(far_g, -2)
    q_grad, src_t = call(
        query_kernel, "vvvv", [out((TOK, HEADS * HD)), out((D, TOK))], "vv", [], 0.1
    )(sg, k_t, src, place)
    kv_grad = (own_g + got_near.astype(F32) + got_far.astype(F32)).astype(BF)
    return (
        q_grad,
        kv_grad[:, :KV],
        kv_grad[:, KV:],
        src_t.T,
        gate_t.T.astype(BF),
        map_grad,
    )


def solution(mesh):
    fine = Mesh(mesh.devices.reshape(8, 2, 8, 2, 2), ALL)
    rows = P(ALL, None)
    fsdp = ("z", "xh", "core")
    return jax.shard_map(
        shards,
        mesh=fine,
        in_specs=(
            rows, rows, rows, P(ALL), rows, rows, rows, rows, rows, P(),
            P(CTX, fsdp, None), P(fsdp, None),
        ),
        out_specs=(rows, rows, rows, rows, rows, P(CTX, fsdp, None)),
        check_vma=False,
    )
```

```python
import jax
import jax.numpy as jnp
from jax import lax
from jax.experimental import pallas as pl
from jax.experimental.pallas import tpu as pltpu
from jax.sharding import Mesh, PartitionSpec as P

TOK = 128
D = 1440
F = 1440
HEADS = 32
KV_HEADS = 4
HD = 64
CAP = 6
CAPP = 8
EXPERTS = 16
ROWS = EXPERTS * CAPP
SEG = 48
SHARD = 45
DP = 1536
HALF = 768
SEND = 3072
BACK = 1664
KV = 256
WIDE = 640
BF = jnp.bfloat16
F32 = jnp.float32
ALL = ("y", "xl", "zh", "zl", "xh", "core")
Z = ("zh", "zl")
CTX = ("y", "xl")
SWAP = ((0, 1), (1, 0))


def dot(a, b, dims):
    return lax.dot_general(a, b, (dims, ((), ())), preferred_element_type=F32)


SPACES = {"s": pltpu.SMEM, "v": pltpu.VMEM, "h": pltpu.HBM}


def out(shape, dtype=BF):
    return jax.ShapeDtypeStruct(shape, dtype)


def call(kernel, ins, outs, out_spaces, scratch, weight_us):
    return pl.pallas_call(
        kernel,
        out_shape=outs,
        in_specs=[pl.BlockSpec(memory_space=SPACES[k]) for k in ins],
        out_specs=[pl.BlockSpec(memory_space=SPACES[k]) for k in out_spaces],
        scratch_shapes=scratch,
        compiler_params=pltpu.CompilerParams(vmem_limit_bytes=60 * 1024 * 1024),
        cost_estimate=pl.CostEstimate(
            flops=0, bytes_accessed=int(weight_us * 3690000), transcendentals=0
        ),
    )


def copies_of(pairs, sems):
    return [pltpu.make_async_copy(a, b, sems.at[i]) for i, (a, b) in enumerate(pairs)]


def order(value, *ties):
    return lax.optimization_barrier((value, *ties))[0]


def dispatch_kernel(
    picked_ref, held_ref, gate_ref, place_ref, x_ref, g_ref, skip_ref, map_ref,
    out_ref, map_out, sent_any, skip_any, sent_ref, skip_s, sems,
):
    held = held_ref[...]
    chosen = [picked_ref[s : s + 1, :] == held for s in range(4)]
    routed = chosen[0] | chosen[1] | chosen[2] | chosen[3]
    routed_f = jnp.where(routed, 1.0, 0.0)
    before = lax.broadcasted_iota(jnp.int32, (TOK, TOK), 0) <= lax.broadcasted_iota(
        jnp.int32, (TOK, TOK), 1
    )
    upper = jnp.where(before, 1.0, 0.0).astype(BF)
    rank = dot(routed_f.astype(BF), upper, ((1,), (0,))) - 1.0
    slot = lax.broadcasted_iota(jnp.int32, (ROWS, TOK), 0) % CAPP
    sent = routed & (rank == slot.astype(F32))
    sent_bf = jnp.where(sent, 1.0, 0.0).astype(BF)
    sent_ref[...] = sent_bf
    copy = pltpu.make_async_copy(sent_ref, sent_any, sems.at[0])
    copy.start()
    gate = jnp.zeros((ROWS, TOK), F32)
    for s in range(4):
        gate = gate + jnp.where(chosen[s] & sent, gate_ref[s : s + 1, :], 0.0)
    gate = jnp.sum(gate, axis=1, keepdims=True)
    rows = dot(sent_bf, x_ref[...], ((1,), (1,))).astype(BF)
    feature = lax.broadcasted_iota(jnp.int32, (D, 256), 0)
    for c in range(DP // 256):
        pick = jnp.where(feature == place_ref[:, c * 256 : (c + 1) * 256], 1.0, 0.0).astype(BF)
        at = slice(c * 256, (c + 1) * 256)
        out_ref[:, at] = dot(rows, pick, ((1,), (0,))).astype(BF)
        map_out[:, at] = dot(map_ref[...], pick, ((1,), (0,))).astype(BF)
        skip_s[:, at] = dot(skip_ref[...], pick, ((0,), (0,))).astype(BF)
    skip_copy = pltpu.make_async_copy(skip_s, skip_any, sems.at[1])
    skip_copy.start()
    grads = dot(sent_bf, g_ref[...], ((1,), (1,))).astype(BF)
    out_ref[:, DP:] = jnp.concatenate(
        [grads, jnp.broadcast_to(gate, (ROWS, SEND - DP - F)).astype(BF)], axis=1
    )
    copy.wait()
    skip_copy.wait()


def shares_kernel(
    q_ref, far_ref, near_ref, own_ref, label_ref, shares_any, qt_any, kt_any, v_any,
    kv_s, bias_s, shares_ref, qt_ref, kt_ref, v_ref, sems,
):
    for part, ref in enumerate((far_ref, near_ref, own_ref)):
        kv_s[part * TOK : (part + 1) * TOK, :] = ref[...]
    marks = kv_s[:, 2 * KV :].astype(F32)
    docs = marks[:, 0:1] * 16.0 + marks[:, 1:2]
    r_at = lax.broadcasted_iota(jnp.int32, (3 * TOK, TOK), 0)
    p_at = lax.broadcasted_iota(jnp.int32, (3 * TOK, TOK), 1)
    allowed = (r_at <= 2 * TOK + p_at) & (docs == label_ref[...])
    bias = jnp.where(allowed, 0.0, -1e30)
    bias_s[...] = jnp.concatenate([bias, bias], axis=1)
    v_ref[...] = kv_s[:, KV : 2 * KV]
    for t in range(2):
        kt_ref[t * 128 : (t + 1) * 128, :] = jnp.transpose(
            kv_s[:, t * 128 : (t + 1) * 128].astype(F32)
        ).astype(BF)
    copies = []
    for g in range(KV_HEADS):
        k_one = kv_s[:, g * HD : (g + 1) * HD]

        def pair(i, carry, g=g, k_one=k_one):
            at = pl.multiple_of((g * 4 + i) * 128, 128)
            flipped = jnp.transpose(q_ref[:, pl.ds(at, 128)].astype(F32) * 0.125).astype(BF)
            qt_ref[pl.ds(at, 128), :] = flipped
            q_two = jnp.concatenate([flipped[:HD], flipped[HD:]], axis=1)
            s = dot(k_one, q_two, ((1,), (0,))) + bias_s[...]
            e = jnp.exp(s - jnp.max(s, axis=0, keepdims=True))
            shares = e * (1.0 / jnp.sum(e, axis=0, keepdims=True))
            shares_ref[:, pl.ds(pl.multiple_of(2 * at, 256), 256)] = shares.astype(BF)
            return carry

        lax.fori_loop(0, 4, pair, 0)
        columns = slice(g * 8 * TOK, (g + 1) * 8 * TOK)
        copies.append(
            pltpu.make_async_copy(
                shares_ref.at[:, columns], shares_any.at[:, columns], sems.at[g]
            )
        )
        copies[-1].start()
    pairs = ((qt_ref, qt_any), (kt_ref, kt_any), (v_ref, v_any))
    for i, (source, target) in enumerate(pairs):
        copies.append(pltpu.make_async_copy(source, target, sems.at[4 + i]))
        copies[-1].start()
    for copy in copies:
        copy.wait()


def activation_grads(pre_ref, grads, gate, pg_ref):
    step = 512
    total = jnp.zeros((pre_ref.shape[0], 1), F32)
    for lo in range(0, DP, step):
        pre = pre_ref[:, lo : lo + step]
        grad = grads(DP + lo, DP + lo + step).astype(F32)
        sig = 1.0 / (1.0 + jnp.exp(-pre))
        total = total + jnp.sum(grad * (pre * sig), axis=1, keepdims=True)
        slope = sig * (1.0 + pre * (1.0 - sig))
        pg_ref[:, lo : lo + step] = (gate * grad * slope).astype(BF)
    return total


def expert_kernel(
    got_ref, wo_ref, wm_any, back_any, pg_any, wm_ref, back_ref, pg_ref, pre_ref, sems
):
    load = pltpu.make_async_copy(wm_any, wm_ref, sems.at[0])
    load.start()
    load.wait()
    for lo in range(0, DP, 512):
        at = slice(lo, lo + 512)
        pre_ref[:, at] = dot(got_ref[:, :HALF], wm_ref[:, at], ((1,), (0,))) + dot(
            got_ref[:, HALF:DP], wo_ref[:, at], ((1,), (0,))
        )
    gate = got_ref[:, DP + F : DP + F + 1].astype(F32)
    total = activation_grads(pre_ref, lambda lo, hi: got_ref[:, lo:hi], gate, pg_ref)
    stores = [pltpu.make_async_copy(pg_ref, pg_any, sems.at[1])]
    stores[0].start()
    pg = pg_ref[...]
    for c in range(HALF // 256):
        r = slice(c * 256, (c + 1) * 256)
        back_ref[:, c * 256 : (c + 1) * 256] = dot(pg, wm_ref[r, :], ((1,), (1,))).astype(BF)
        back_ref[:, HALF + c * 256 : HALF + (c + 1) * 256] = dot(
            pg, wo_ref[r, :], ((1,), (1,))
        ).astype(BF)
    back_ref[:, DP:] = jnp.broadcast_to(total, (ROWS, BACK - DP)).astype(BF)
    stores.append(pltpu.make_async_copy(back_ref, back_any, sems.at[2]))
    stores[1].start()
    for copy in stores:
        copy.wait()


def map_kernel(
    at_ref, wm_any, wo_any, own_any, near_any, core_any, far_any, pg_any, part_any,
    wm_ref, wo_ref, own_ref, near_ref, core_ref, far_ref, own_pg_ref, pg_ref, pre_ref, part_ref,
    sems,
):
    pairs = (
        (near_any, near_ref), (core_any, core_ref), (far_any, far_ref), (wm_any, wm_ref),
        (wo_any, wo_ref), (own_any, own_ref), (pg_any, own_pg_ref),
    )
    loads = copies_of(pairs, sems)
    for copy in loads:
        copy.start()
    for copy in loads:
        copy.wait()

    def columns(lo, hi):
        return jnp.concatenate(
            [near_ref[:, lo:hi], core_ref[:, lo:hi], far_ref[:, lo:hi]], axis=0
        )

    first, second = slice(0, HALF), slice(HALF, DP)
    x_mine = jnp.concatenate([near_ref[:, first], core_ref[:, second], far_ref[:, second]], axis=0)
    x_other = jnp.concatenate([near_ref[:, second], core_ref[:, first], far_ref[:, first]], axis=0)
    for lo in range(0, DP, 512):
        at = slice(lo, lo + 512)
        pre_ref[:, at] = dot(x_mine, wm_ref[:, at], ((1,), (0,))) + dot(
            x_other, wo_ref[:, at], ((1,), (0,))
        )
    gate = columns(DP + F, DP + F + 1).astype(F32)
    activation_grads(pre_ref, columns, gate, pg_ref)
    pg = jnp.concatenate([own_pg_ref[...], pg_ref[...]], axis=0)
    for c in range(HALF // 256):
        r = slice(c * 256, (c + 1) * 256)
        x = jnp.concatenate([own_ref[:, r], x_mine[:, r]], axis=0)
        part_ref[r, :] = dot(x, pg, ((0,), (0,))).astype(BF)
    stores = []
    for k in range(4):
        rows = pl.ds(pl.multiple_of((2 * k + at_ref[2]) * 2 * SEG, 2 * SEG), 2 * SEG)
        stores.append(
            pltpu.make_async_copy(
                part_ref.at[rows, :], part_any.at[k * 2 * SEG : (k + 1) * 2 * SEG, :],
                sems.at[7 + k],
            )
        )
        stores[-1].start()
    for copy in stores:
        copy.wait()


def combine_kernel(
    picked_ref, held_ref, back_any, sent_any, skip_any, om_any,
    gate_ref, src_ref, hidden_ref, cot_ref, back_ref, sent_ref, skip_ref, om_ref, sems,
):
    pairs = (
        (sent_any, sent_ref), (skip_any, skip_ref), (om_any, om_ref), (back_any, back_ref)
    )
    copies = copies_of(pairs, sems)
    for copy in copies:
        copy.start()
    copies[3].wait()
    copies[0].wait()
    sent_bf = sent_ref[...]
    sent = sent_bf.astype(F32) > 0.5
    held = held_ref[...]
    gate_part = back_ref[:, DP : DP + 1].astype(F32)
    for s in range(4):
        mine = (picked_ref[s : s + 1, :] == held) & sent
        gate_ref[s : s + 1, :] = jnp.sum(jnp.where(mine, gate_part, 0.0), axis=0, keepdims=True)
    src = dot(sent_bf, back_ref[:, :DP], ((0,), (0,))).astype(BF)
    src_ref[...] = src
    copies[1].wait()
    hidden = (skip_ref[...].astype(F32) + src.astype(F32)).astype(BF)
    hidden_ref[...] = hidden
    copies[2].wait()
    for c in range(4):
        rows = slice(c * 256, (c + 1) * 256)
        cot_ref[rows, :] = dot(om_ref[rows, :], hidden, ((1,), (1,))).astype(BF)


def late_kernel(
    at_ref, cotm_ref, hidden_ref, v_any, oo_any, qt_any, shares_any,
    sg_ref, farg_ref, nearg_ref, owng_ref,
    cot_s, acck_s, accv_s, v_ref, oo_ref, qt_ref, shares_ref, sems,
):
    pairs = ((oo_any, oo_ref), (v_any, v_ref), (qt_any, qt_ref), (shares_any, shares_ref))
    copies = copies_of(pairs, sems)
    for copy in copies:
        copy.start()
    core, xh = at_ref[0], at_ref[1]

    def spread(block, c, place):
        for j in range(4):
            across = xh if j % 2 == 0 else 1 - xh
            at = pl.multiple_of((c * 2 + j // 2) * 256 + across * 128 + place, HD)
            cot_s[pl.ds(at, HD), :] = block[j * HD : (j + 1) * HD]

    for c in range(4):
        spread(cotm_ref[c * 256 : (c + 1) * 256, :], c, core * HD)
    hidden = jnp.concatenate([hidden_ref[:, HALF:], hidden_ref[:, :HALF]], axis=1)
    copies[0].wait()
    for c in range(4):
        rows = slice(c * 256, (c + 1) * 256)
        spread(dot(oo_ref[rows, :], hidden, ((1,), (1,))).astype(BF), c, HD - core * HD)

    for copy in copies[1:]:
        copy.wait()
    for t in range(2):
        sums = []
        for g in (2 * t, 2 * t + 1):
            v_one = v_ref[:, g * HD : (g + 1) * HD]
            for i in range(4):
                n = g * 4 + i
                rows = slice(n * 128, n * 128 + HD), slice(n * 128 + HD, (n + 1) * 128)
                q_two = jnp.concatenate([qt_ref[rows[0], :], qt_ref[rows[1], :]], axis=1)
                c_two = jnp.concatenate([cot_s[rows[0], :], cot_s[rows[1], :]], axis=1)
                low = shares_ref[:, n * 256 : (n + 1) * 256]
                dp = dot(v_one, c_two, ((1,), (0,)))
                shares = low.astype(F32)
                centre = jnp.sum(shares * dp, axis=0, keepdims=True)
                sg = (shares * (dp - centre)).astype(BF)
                sg_ref[:, n * 256 : (n + 1) * 256] = sg
                ak = dot(sg, q_two, ((1,), (1,)))
                av = dot(low, c_two, ((1,), (1,)))
                if i == 0:
                    acck_s[...] = ak
                    accv_s[...] = av
                else:
                    acck_s[...] += ak
                    accv_s[...] += av
            sums.append((acck_s[...], accv_s[...]))
        for kind in range(2):
            tile = jnp.concatenate([sums[0][kind], sums[1][kind]], axis=1)
            at = slice(kind * KV + t * 128, kind * KV + (t + 1) * 128)
            farg_ref[:, at] = tile[:TOK].astype(BF)
            nearg_ref[:, at] = tile[TOK : 2 * TOK].astype(BF)
            owng_ref[:, at] = tile[2 * TOK :]


def query_kernel(sg_ref, kt_ref, src_ref, place_ref, qg_ref, out_ref):
    for n in range(16):
        g = n // 4
        qg = dot(kt_ref[g * HD : (g + 1) * HD, :], sg_ref[:, n * 256 : (n + 1) * 256], ((1,), (0,)))
        both = jnp.concatenate([qg[:, :TOK], qg[:, TOK:]], axis=0) * 0.125
        qg_ref[:, n * 128 : (n + 1) * 128] = jnp.transpose(both).astype(BF)
    feature = lax.broadcasted_iota(jnp.int32, (D, 256), 0)
    total = jnp.zeros((D, TOK), F32)
    for c in range(DP // 256):
        at = slice(c * 256, (c + 1) * 256)
        pick = jnp.where(feature == place_ref[:, at], 1.0, 0.0).astype(BF)
        total = total + dot(pick, src_ref[:, at], ((1,), (1,)))
    out_ref[...] = total.astype(BF)


def both_xh(piece):
    other = lax.ppermute(piece, "xh", SWAP)
    lower = lax.axis_index("xh") == 0
    return jnp.concatenate(
        [jnp.where(lower, piece, other), jnp.where(lower, other, piece)], axis=0
    )


def shift_blocks(value, steps):
    first, last = max(0, -steps), min(512, 512 - steps)
    return lax.ppermute(value, ALL, [(i, i + steps) for i in range(first, last)])


def shards(q, keys, values, label, skip, x, g, picked, mix, retained, weights, out_map):
    core = lax.axis_index("core")
    xh = lax.axis_index("xh")
    w_pad = jnp.pad(weights[0], ((0, SEG - SHARD), (0, DP - F)))
    w_pair = both_xh(w_pad)
    w_mine = lax.all_gather(w_pair, Z, axis=0, tiled=True)

    plus = (label + 1).astype(jnp.int32)
    marks = jnp.stack([plus // 16, plus % 16], axis=1).astype(BF)
    own = jnp.concatenate(
        [keys, values, jnp.pad(marks, ((0, 0), (0, WIDE - 2 * KV - 2)))], axis=1
    )
    picked_t = order(picked.T, w_pair)
    held = jnp.repeat(retained[:EXPERTS], CAPP)[:, None]
    column = jnp.arange(DP, dtype=jnp.int32)
    half = column // HALF
    rest = column % HALF
    within = rest % SEG
    pair = rest // SEG
    owner = (pair // 2) * 4 + (pair % 2) * 2 + (half ^ core)
    place = jnp.where(within < SHARD, owner * SHARD + within, -1)[None, :]
    dma = pltpu.SemaphoreType.DMA
    send, o_placed, sent, skip_placed = call(
        dispatch_kernel,
        "vvvvvvvv",
        [out((ROWS, SEND)), out((HD, DP)), out((ROWS, TOK)), out((TOK, DP))],
        "vvhh",
        [pltpu.VMEM((ROWS, TOK), BF), pltpu.VMEM((TOK, DP), BF), dma((2,))],
        2,
    )(picked_t, held, mix.astype(F32).T, place, x.T, g.T, skip.T, out_map)
    got = lax.all_to_all(send.reshape(EXPERTS, CAPP, SEND), CTX, 0, 0, tiled=True)
    own = order(own, send)
    near = shift_blocks(own, 1)
    far = shift_blocks(own, 2)
    o_across = lax.ppermute(o_placed, "xh", SWAP)
    near, far, o_across, got = lax.optimization_barrier((near, far, o_across, got))
    shares_shape, qt_shape = (3 * TOK, HEADS * TOK), (HEADS * HD, TOK)
    kt_shape, v_shape = (KV, 3 * TOK), (3 * TOK, KV)
    shares, q_t, k_t, v_win = call(
        shares_kernel,
        "vvvvv",
        [out(shares_shape), out(qt_shape), out(kt_shape), out(v_shape)],
        "hhhh",
        [
            pltpu.VMEM((3 * TOK, WIDE), BF),
            pltpu.VMEM((3 * TOK, 2 * TOK), F32),
            pltpu.VMEM(shares_shape, BF),
            pltpu.VMEM(qt_shape, BF),
            pltpu.VMEM(kt_shape, BF),
            pltpu.VMEM(v_shape, BF),
            dma((7,)),
        ],
        8,
    )(q, far, near, own, plus.astype(F32)[None, :])

    got = got.reshape(ROWS, SEND)
    got_near = lax.ppermute(got, "zl", SWAP)
    got_core = lax.ppermute(order(got, v_win), "core", SWAP)
    o_pair = jnp.concatenate([o_placed, o_across], axis=0)
    o_mine = lax.all_gather(o_pair, Z, axis=0, tiled=True)
    w_mine = order(w_mine, got_core, o_pair)
    w_other = lax.ppermute(w_mine, "core", SWAP)
    spot = jnp.stack([core, xh, lax.axis_index("zl")]).astype(jnp.int32)
    back, pg = call(
        expert_kernel,
        "vvh",
        [out((ROWS, BACK)), out((ROWS, DP))],
        "hh",
        [
            pltpu.VMEM((HALF, DP), BF),
            pltpu.VMEM((ROWS, BACK), BF),
            pltpu.VMEM((ROWS, DP), BF),
            pltpu.VMEM((ROWS, DP), F32),
            dma((3,)),
        ],
        3,
    )(got, w_other, w_mine)
    got_far = lax.ppermute(order(got_near, pg), "core", SWAP)
    returned = lax.all_to_all(back.reshape(EXPERTS, CAPP, BACK), CTX, 0, 0, tiled=True)
    returned = returned.reshape(ROWS, BACK)
    partial = call(
        map_kernel,
        "shhhhhhh",
        [out((HALF // 2, DP))],
        "h",
        [
            pltpu.VMEM((HALF, DP), BF),
            pltpu.VMEM((HALF, DP), BF),
            pltpu.VMEM((ROWS, SEND), BF),
            pltpu.VMEM((ROWS, SEND), BF),
            pltpu.VMEM((ROWS, SEND), BF),
            pltpu.VMEM((ROWS, SEND), BF),
            pltpu.VMEM((ROWS, DP), BF),
            pltpu.VMEM((3 * ROWS, DP), BF),
            pltpu.VMEM((3 * ROWS, DP), F32),
            pltpu.VMEM((HALF, DP), BF),
            dma((11,)),
        ],
        8,
    )(spot, w_mine, w_other, got, got_near, got_core, got_far, pg)[0]
    partial = order(partial, returned)
    terms = lax.all_to_all(partial.reshape(8, SEG, DP), ("zh", "xh"), 0, 0, tiled=True)
    o_mine = order(o_mine, returned, partial)
    o_other = lax.ppermute(o_mine, "core", SWAP)
    half_shape = (16 * HD, DP)
    gate_t, src, hidden, cot_mine = call(
        combine_kernel,
        "vvhhhh",
        [out((4, TOK), F32), out((TOK, DP)), out((TOK, DP)), out((16 * HD, TOK))],
        "vvvv",
        [
            pltpu.VMEM((ROWS, BACK), BF),
            pltpu.VMEM((ROWS, TOK), BF),
            pltpu.VMEM((TOK, DP), BF),
            pltpu.VMEM(half_shape, BF),
            dma((4,)),
        ],
        3,
    )(picked_t, held, returned, sent, skip_placed, o_mine)
    sg, far_g, near_g, own_g = call(
        late_kernel,
        "svvhhhh",
        [
            out(shares_shape),
            out((TOK, 2 * KV)),
            out((TOK, 2 * KV)),
            out((TOK, 2 * KV), F32),
        ],
        "vvvv",
        [
            pltpu.VMEM((HEADS * HD, TOK), BF),
            pltpu.VMEM((3 * TOK, HD), F32),
            pltpu.VMEM((3 * TOK, HD), F32),
            pltpu.VMEM(v_shape, BF),
            pltpu.VMEM(half_shape, BF),
            pltpu.VMEM(qt_shape, BF),
            pltpu.VMEM(shares_shape, BF),
            dma((4,)),
        ],
        0.1,
    )(spot, cot_mine, hidden, v_win, o_other, q_t, shares)
    got_next = shift_blocks(near_g, -1)
    got_last = shift_blocks(far_g, -2)
    terms = order(terms, got_next, got_last)
    map_grad = jnp.sum(terms.astype(F32), axis=0)[None, :SHARD, :F].astype(BF)
    q_grad, src_t = call(
        query_kernel, "vvvv", [out((TOK, HEADS * HD)), out((D, TOK))], "vv", [], 0.1
    )(sg, k_t, src, place)
    kv_grad = (own_g + got_next.astype(F32) + got_last.astype(F32)).astype(BF)
    return (
        q_grad,
        kv_grad[:, :KV],
        kv_grad[:, KV:],
        src_t.T,
        gate_t.T.astype(BF),
        map_grad,
    )


def solution(mesh):
    fine = Mesh(mesh.devices.reshape(8, 2, 4, 2, 2, 2), ALL)
    rows = P(ALL, None)
    fsdp = ("zh", "zl", "xh", "core")
    return jax.shard_map(
        shards,
        mesh=fine,
        in_specs=(
            rows, rows, rows, P(ALL), rows, rows, rows, rows, rows, P(),
            P(CTX, fsdp, None), P(fsdp, None),
        ),
        out_specs=(rows, rows, rows, rows, rows, P(CTX, fsdp, None)),
        check_vma=False,
    )
```
